32 devices in a mesh: row: 4 (over y, x), col: 8 (over z, core).
Axes of the slice: x: 2, y: 2, z: 4, core: 2. Of those that a mesh axis runs over, the one named last changes fastest.
Arguments:
- r_vector: bfloat16 [3072, 18432], P(('row', 'col')), may hold values from -100 to 100, as said below
- r_previous: bfloat16 [3072, 18432], P(('row', 'col')), may hold values from -100 to 100, as said below
- cycle_block: bfloat16 [18432, 18432], P('row', 'col'), may hold values from -0.046875 to 0.046875
- ladder_block: bfloat16 [48, 48, 48, 48], P(None, 'col', None, 'row'), may hold values from -0.125 to 0.125
- occ_energy: float32 [48], replicated, may hold values from -3 to -0.5
- vir_energy: float32 [384], replicated, may hold values from 0.3 to 4
- beta_previous: float32 [64], replicated, may hold values from 0.3 to 3
Outputs:
- next_vector: bfloat16 [3072, 18432], P(('row', 'col'))
- alpha_coef: float32 [64], replicated
- beta_coef: float32 [64], replicated
The draws below stay inside these ranges and needn't reach their ends.
Inputs may be any that keep to these rules, and one draw needn't show every extreme that they name: `r_vector`: real-valued amplitudes, rough from entry to entry. `r_previous`: real-valued amplitudes, rough from entry to entry.
All inputs are finite; a program needn't handle non-finite values.
Results may differ from the reference program's by a relative error of at most 0.001.
Values may be sent and summed in bfloat16 or wider, within the bound.
No kernel may reach another device: no remote copies, remote signals or barrier semaphores. Data moves between devices by JAX's collectives and lax.ppermute only.
A program may use at most 192 MiB of HBM per device.

```python
import math
import jax
import jax.numpy as jnp
from jax import lax

O = 48
V = 384
NVEC = 64


def scaled_vector(key):
    key_base, key_rows, key_cols = jax.random.split(key, 3)
    row_count = NVEC * O
    col_count = O * V
    position = (jnp.arange(row_count) % O).astype(jnp.float32) / (O - 1)
    row_scale = jnp.exp(jnp.log(10.0) * jax.random.uniform(key_rows, (row_count,))) * jnp.exp(jnp.log(3.0) * position)
    col_scale = jnp.exp(jnp.log(10.0) * jax.random.uniform(key_cols, (col_count,)))
    base_draw = jnp.clip(jax.random.normal(key_base, (row_count, col_count)), -4.0, 4.0)
    return (base_draw * row_scale[:, None] * col_scale[None, :] / 12.0).astype(jnp.bfloat16)


def draw_r_vector(key, part):
    return scaled_vector(jax.random.fold_in(key, 11))


def draw_r_previous(key, part):
    return scaled_vector(jax.random.fold_in(key, 23))


def shard_levels(stream_key, extent, pieces, smallest, largest):
    def one(axis_at, shards_of):
        steps = jax.random.uniform(jax.random.fold_in(jax.random.fold_in(stream_key, 6), axis_at), (shards_of,), jnp.float32, smallest / len(pieces), largest / len(pieces))
        return jnp.repeat(jnp.exp(steps), extent[axis_at] // shards_of).reshape((-1,) + (1,) * (len(extent) - axis_at - 1))

    factor_of = one(*pieces[0])
    for cut in pieces[1:]:
        factor_of = factor_of * one(*cut)
    return factor_of


def noise(rng, dims, scale, reach, shards=(), kind=jnp.bfloat16):
    entries = jax.random.normal(rng, dims, jnp.float32) * scale
    if len(shards) > 0:
        entries = shard_levels(rng, dims, shards, -0.22, 0.18) * entries
    return jnp.clip(entries, min=-reach, max=reach).astype(kind)


def setup_inputs(seed: int = 0) -> dict:
    arg_keys = jax.random.split(jax.random.key(seed), 8)
    r_vector = draw_r_vector(jax.random.fold_in(arg_keys[7], 71), 0)
    r_previous = draw_r_previous(jax.random.fold_in(arg_keys[7], 71), 0)
    cycle_block = noise(arg_keys[2], (O * V, O * V), (O * V) ** -0.5, 0.046875, ((0, 4), (1, 8)))
    ladder_block = noise(arg_keys[3], (O, O, O, O), (O * O) ** -0.5, 0.125, ((1, 8), (3, 4)))
    occ_energy = jnp.clip(jax.random.uniform(arg_keys[4], (O,), jnp.float32, -3.0, -0.5), -3.0, -0.5)
    vir_energy = jnp.clip(jnp.exp(jax.random.uniform(arg_keys[5], (V,), jnp.float32, math.log(0.3), math.log(4.0))), 0.3, 4.0)
    beta_previous = jnp.clip(jnp.exp(jax.random.uniform(arg_keys[6], (NVEC,), jnp.float32, math.log(0.3), math.log(3.0))), 0.3, 3.0)
    return {"r_vector": r_vector, "r_previous": r_previous, "cycle_block": cycle_block, "ladder_block": ladder_block, "occ_energy": occ_energy, "vir_energy": vir_energy, "beta_previous": beta_previous}


def per_vector(values):
    return lax.optimization_barrier(jnp.sum(values.reshape(NVEC, -1), axis=1))

def reference(r_vector, r_previous, cycle_block, ladder_block, occ_energy, vir_energy, beta_previous):
    row_count = NVEC * O
    r_float = r_vector.astype(jnp.float32)
    prev_float = r_previous.astype(jnp.float32)
    cycle_part = jnp.dot(r_float, cycle_block.astype(jnp.float32), precision=lax.Precision.HIGHEST)
    cube = r_float.reshape(NVEC, O, O, V)
    ladder_part = jnp.einsum('ijpq,npqa->nija', ladder_block.astype(jnp.float32), cube, precision=lax.Precision.HIGHEST).reshape(row_count, O * V)
    diagonal = vir_energy[None, None, None, :] - occ_energy[None, :, None, None] - occ_energy[None, None, :, None]
    sigma_rows = cycle_part + ladder_part + (diagonal * cube).reshape(row_count, O * V)
    count_all = O * O * V
    rs_sum = per_vector(r_float * sigma_rows)
    rr_sum = per_vector(r_float * r_float)
    alpha_coef = rs_sum / count_all / (rr_sum / count_all + 1e-06)
    residual_vec = sigma_rows - jnp.repeat(alpha_coef, O)[:, None] * r_float - jnp.repeat(beta_previous, O)[:, None] * prev_float
    beta_coef = jnp.sqrt(per_vector(residual_vec * residual_vec) / count_all + 1e-06)
    next_vector = (residual_vec / jnp.repeat(beta_coef, O)[:, None]).astype(jnp.bfloat16)
    return (next_vector, alpha_coef, beta_coef)
```

```python
import functools

import jax
import jax.numpy as jnp
from jax import lax
from jax.experimental import pallas as pl
from jax.experimental.pallas import tpu as pltpu
from jax.sharding import PartitionSpec as P

O = 48
V = 384
NVEC = 64
CORES = 2
AXES = ("row", "col")
POWER = 16
FLOOR = 2.0**-7.75
PART_GAIN = 16.0
SUM_GAIN = 8.0


def encode(value, gain):
    size = jnp.abs(value) * gain + FLOOR
    size = size * size
    size = size * size
    size = size * size
    size = size * size
    return jnp.where(value < 0, -size, size).astype(jnp.bfloat16)


def decode(code, gain):
    wide = code.astype(jnp.float32)
    size = (jnp.exp2(jnp.log2(jnp.abs(wide)) * (1.0 / POWER)) - FLOOR) * (1.0 / gain)
    return jnp.where(wide < 0, -size, size)


def product_kernel(coded, mine_ref, other_ref, cycle_ref, ladder_ref, out_ref, rows_buf, ladder_buf, sems):
    step = pl.program_id(0)
    half, depth = mine_ref.shape
    vectors = 2 * half // O
    width = cycle_ref.shape[1]
    q_part = depth // V
    j_part = ladder_ref.shape[0] // O

    @pl.when(step == 0)
    def _():
        first = pltpu.make_async_copy(mine_ref, rows_buf.at[pl.ds(0, half)], sems.at[0])
        second = pltpu.make_async_copy(other_ref, rows_buf.at[pl.ds(half, half)], sems.at[1])
        first.start()
        second.start()
        first.wait()
        second.wait()
        for n in range(vectors):
            stacked = jnp.concatenate(
                [rows_buf[n * O : (n + 1) * O, q * V : (q + 1) * V] for q in range(q_part)], axis=0
            )
            term = jnp.dot(ladder_ref[...], stacked, preferred_element_type=jnp.float32)
            for j in range(j_part):
                ladder_buf[n * O : (n + 1) * O, j * V : (j + 1) * V] = term[j * O : (j + 1) * O]

    start = pl.multiple_of(step * width, width)
    value = jnp.dot(rows_buf[...], cycle_ref[...], preferred_element_type=jnp.float32)
    value = value + ladder_buf[:, pl.ds(start, width)]
    if coded:
        out_ref[...] = encode(value, PART_GAIN)
    else:
        out_ref[...] = value


def product(mine, other, cycle_block, ladder_rows, coded):
    half, depth = mine.shape
    out_width = cycle_block.shape[1]
    width = 2 * V if out_width % (2 * V) == 0 else V
    flops = 2 * 2 * half * depth * out_width
    return pl.pallas_call(
        functools.partial(product_kernel, coded),
        grid=(out_width // width,),
        in_specs=[
            pl.BlockSpec(memory_space=pl.ANY),
            pl.BlockSpec(memory_space=pl.ANY),
            pl.BlockSpec((depth, width), lambda i: (0, i)),
            pl.BlockSpec(ladder_rows.shape, lambda i: (0, 0)),
        ],
        out_specs=pl.BlockSpec((2 * half, width), lambda i: (0, i)),
        out_shape=jax.ShapeDtypeStruct((2 * half, out_width), jnp.bfloat16 if coded else jnp.float32),
        scratch_shapes=[
            pltpu.VMEM((2 * half, depth), jnp.bfloat16),
            pltpu.VMEM((2 * half, out_width), jnp.float32),
            pltpu.SemaphoreType.DMA((2,)),
        ],
        compiler_params=pltpu.CompilerParams(vmem_limit_bytes=40 * 1024 * 1024),
        cost_estimate=pl.CostEstimate(
            flops=flops, bytes_accessed=2 * depth * out_width, transcendentals=0
        ),
    )(mine, other, cycle_block, ladder_rows)


def power_of_two(exponent):
    return jnp.exp2(exponent).astype(jnp.bfloat16)


def streamed(
    r_vector, r_previous, cycle_block, ladder_block, occ_energy, vir_energy, beta_previous
):
    n_row = lax.axis_size("row")
    n_col = lax.axis_size("col")
    n_chip = n_col // CORES
    local_rows, row_width = r_vector.shape
    depth = row_width // n_row
    out_width = cycle_block.shape[1]
    j_part = ladder_block.shape[1]
    q_part = ladder_block.shape[3]
    row_at = lax.axis_index("row")
    col_at = lax.axis_index("col")
    chip_at = col_at // CORES
    core_at = col_at % CORES
    order = list(range(0, n_chip, 2)) + list(range(1, n_chip, 2))[::-1]
    place = [order.index(chip) for chip in range(n_chip)]
    paired = n_row & (n_row - 1) == 0

    def partner(row, m):
        return row ^ m if paired else (row + m) % n_row

    def back(row, m):
        return row ^ m if paired else (row + n_row - m) % n_row

    def send(value, rows=0, hops=0, swap=0, reverse=False):
        pairs = []
        for row in range(n_row):
            for chip in range(n_chip):
                for core in range(CORES):
                    to_row = back(row, rows) if reverse else partner(row, rows)
                    to_chip = order[(place[chip] + hops) % n_chip]
                    to_core = (core + swap) % CORES
                    pairs.append(
                        (
                            row * n_col + chip * CORES + core,
                            to_row * n_col + to_chip * CORES + to_core,
                        )
                    )
        return lax.ppermute(value, AXES, pairs)

    ladder_rows = ladder_block.transpose(1, 0, 3, 2).reshape(j_part * O, q_part * O)

    vectors = local_rows // O
    r_float = r_vector.astype(jnp.float32)
    rr_sum = jnp.sum(r_float.reshape(vectors, O * row_width) ** 2, axis=1)
    exponent = jnp.clip(jnp.floor(0.5 * jnp.log2(jnp.maximum(rr_sum, 1e-37))), -60.0, 60.0)
    shrink = jnp.repeat(power_of_two(-exponent), O)
    grow = jnp.repeat(power_of_two(exponent), O).astype(jnp.float32)

    def own_part(m):
        at = partner(row_at, m) * depth
        return lax.dynamic_slice_in_dim(r_vector, at, depth, axis=1) * shrink[:, None]

    held = [own_part(0)]
    for m in range(1, n_row):
        held.append(send(own_part(m), rows=m))
    received = []
    for s in range(n_chip):
        if s > 0:
            held = [send(part, hops=1) for part in held]
        turn = list(range(1, n_row)) + [0] if s > 0 else list(range(n_row))
        total = None
        parts = {}
        for m in turn:
            other = send(held[m], swap=1)
            parts[m] = product(held[m], other, cycle_block, ladder_rows, m != 0)
        total = parts[0]
        for m in range(1, n_row):
            arrived = send(parts[m], rows=m, reverse=True)
            total = total + decode(arrived, PART_GAIN)
        if s == 0:
            received.append(total[:local_rows])
            received.append(send(total[local_rows:], swap=1))
        else:
            code = encode(total, SUM_GAIN)
            for swap in range(CORES):
                block = code[swap * local_rows : (swap + 1) * local_rows]
                received.append(decode(send(block, hops=n_chip - s, swap=swap), SUM_GAIN))

    order_table = jnp.array(order, dtype=jnp.int32)
    place_at = jnp.array(place, dtype=jnp.int32)[chip_at]
    starts = []
    for s in range(n_chip):
        for swap in range(CORES):
            chip = order_table[(place_at + s) % n_chip]
            starts.append((chip * CORES + (core_at + swap) % CORES) * out_width)

    def blocks_of(array):
        return [lax.dynamic_slice_in_dim(array, at, out_width, axis=1) for at in starts]

    r_blocks = blocks_of(r_vector)
    prev_blocks = blocks_of(r_previous)
    count_all = O * O * V
    linear_index = row_at * n_col + col_at
    occ_tile = jnp.tile(occ_energy, vectors)
    sigma_blocks = []
    for at, block, value in zip(starts, r_blocks, received):
        occ_here = lax.dynamic_slice_in_dim(occ_energy, at // V, j_part)
        diagonal = vir_energy[None, None, :] - occ_tile[:, None, None] - occ_here[None, :, None]
        sigma_blocks.append(
            value * grow[:, None]
            + diagonal.reshape(local_rows, out_width) * block.astype(jnp.float32)
        )

    def per_vector(values):
        return sum(jnp.sum(v.reshape(vectors, O * out_width), axis=1) for v in values)

    rs_sum = per_vector([s * b.astype(jnp.float32) for s, b in zip(sigma_blocks, r_blocks)])
    alpha = rs_sum / count_all / (rr_sum / count_all + 1e-06)
    beta_here = lax.dynamic_slice_in_dim(beta_previous, linear_index * vectors, vectors)
    alpha_rows = jnp.repeat(alpha, O)[:, None]
    beta_rows = jnp.repeat(beta_here, O)[:, None]
    residual = [
        s - alpha_rows * b.astype(jnp.float32) - beta_rows * p.astype(jnp.float32)
        for s, b, p in zip(sigma_blocks, r_blocks, prev_blocks)
    ]
    beta = jnp.sqrt(per_vector([v * v for v in residual]) / count_all + 1e-06)
    next_vector = jnp.zeros((local_rows, row_width), jnp.bfloat16)
    for at, v in zip(starts, residual):
        next_vector = lax.dynamic_update_slice_in_dim(
            next_vector, (v / jnp.repeat(beta, O)[:, None]).astype(jnp.bfloat16), at, axis=1
        )
    both = jnp.zeros((2, NVEC), jnp.float32)
    both = lax.dynamic_update_slice(both, jnp.stack([alpha, beta]), (0, linear_index * vectors))
    both = lax.psum(both, AXES)
    return (next_vector, both[0], both[1])


def gathered(
    r_vector, r_previous, cycle_block, ladder_block, occ_energy, vir_energy, beta_previous
):
    n_row = lax.axis_size("row")
    n_col = lax.axis_size("col")
    local_rows = r_vector.shape[0]
    row_width = r_vector.shape[1]
    all_rows = NVEC * O
    j_part = ladder_block.shape[1]
    q_part = ladder_block.shape[3]
    column_part = lax.all_to_all(r_vector, "row", split_axis=1, concat_axis=0, tiled=True)
    shaped = column_part.reshape(n_row, 1, local_rows, column_part.shape[1])
    gathered = lax.all_gather(shaped, "col", axis=1, tiled=True)
    operand = gathered.reshape(all_rows, column_part.shape[1])
    cycle_part = jnp.dot(operand, cycle_block, preferred_element_type=jnp.float32)
    ladder_part = jnp.einsum(
        "ijpq,npqa->nija",
        ladder_block,
        operand.reshape(NVEC, O, q_part, V),
        preferred_element_type=jnp.float32,
    )
    out_width = j_part * V
    partial_value = cycle_part + ladder_part.reshape(all_rows, out_width)
    summed = lax.psum_scatter(
        partial_value.reshape(n_row, n_col, local_rows, out_width),
        "row",
        scatter_dimension=0,
        tiled=True,
    )
    sigma_rows = lax.all_to_all(summed, "col", split_axis=1, concat_axis=3, tiled=True)
    sigma_rows = sigma_rows.reshape(local_rows, row_width)
    linear_index = lax.axis_index("row") * n_col + lax.axis_index("col")
    row_ids = linear_index * local_rows + jnp.arange(local_rows, dtype=jnp.int32)
    occ_index = row_ids % O
    vec_of_row = row_ids // O
    occ_rows = jnp.sum(
        jnp.where(occ_index[:, None] == jnp.arange(O)[None, :], occ_energy[None, :], 0.0), axis=1
    )
    r_float = r_vector.astype(jnp.float32)
    prev_float = r_previous.astype(jnp.float32)
    diagonal = vir_energy[None, None, :] - occ_rows[:, None, None] - occ_energy[None, :, None]
    sigma_rows = sigma_rows + (diagonal * r_float.reshape(local_rows, O, V)).reshape(
        local_rows, row_width
    )
    member = (vec_of_row[:, None] == jnp.arange(NVEC)[None, :]).astype(jnp.float32)
    count_all = O * O * V

    def per_vector(row_sums):
        return jnp.sum(member * row_sums[:, None], axis=0)

    def per_row(coefs):
        return jnp.sum(member * coefs[None, :], axis=1)

    ss_sum, rs_sum, rr_sum, sp_sum, rp_sum, pp_sum = lax.psum(
        (
            per_vector(jnp.sum(sigma_rows * sigma_rows, axis=1)),
            per_vector(jnp.sum(r_float * sigma_rows, axis=1)),
            per_vector(jnp.sum(r_float * r_float, axis=1)),
            per_vector(jnp.sum(prev_float * sigma_rows, axis=1)),
            per_vector(jnp.sum(r_float * prev_float, axis=1)),
            per_vector(jnp.sum(prev_float * prev_float, axis=1)),
        ),
        AXES,
    )
    alpha_coef = rs_sum / count_all / (rr_sum / count_all + 1e-06)
    norm_sum = (
        ss_sum
        - 2.0 * alpha_coef * rs_sum
        - 2.0 * beta_previous * sp_sum
        + alpha_coef * alpha_coef * rr_sum
        + 2.0 * alpha_coef * beta_previous * rp_sum
        + beta_previous * beta_previous * pp_sum
    )
    residual_vec = (
        sigma_rows
        - per_row(alpha_coef)[:, None] * r_float
        - per_row(beta_previous)[:, None] * prev_float
    )
    beta_coef = jnp.sqrt(norm_sum / count_all + 1e-06)
    next_vector = (residual_vec / per_row(beta_coef)[:, None]).astype(jnp.bfloat16)
    return (next_vector, alpha_coef, beta_coef)


def on_device(r_vector, *others):
    whole_vectors = r_vector.shape[0] % O == 0 and lax.axis_size("col") % CORES == 0
    body = streamed if whole_vectors else gathered
    return body(r_vector, *others)


def solution(mesh):
    placed = (
        P(AXES, None),
        P(AXES, None),
        P("row", "col"),
        P(None, "col", None, "row"),
        P(),
        P(),
        P(),
    )
    return jax.shard_map(
        on_device,
        mesh=mesh,
        in_specs=placed,
        out_specs=(P(AXES, None), P(), P()),
        check_vma=False,
    )
```

```python
import functools

import jax
import jax.numpy as jnp
from jax import lax
from jax.experimental import pallas as pl
from jax.experimental.pallas import tpu as pltpu
from jax.sharding import PartitionSpec as P

O = 48
V = 384
NVEC = 64
CORES = 2
AXES = ("row", "col")
POWER = 16
FLOOR = 2.0**-7.75
PART_GAIN = 16.0
SUM_GAIN = 8.0


def encode(value, gain):
    size = jnp.abs(value) * gain + FLOOR
    size = size * size
    size = size * size
    size = size * size
    size = size * size
    return jnp.where(value < 0, -size, size).astype(jnp.bfloat16)


def decode(code, gain):
    wide = code.astype(jnp.float32)
    size = (jnp.exp2(jnp.log2(jnp.abs(wide)) * (1.0 / POWER)) - FLOOR) * (1.0 / gain)
    return jnp.where(wide < 0, -size, size)


def product_kernel(coded, *refs):
    count = len(coded)
    parts = refs[:count]
    own_ref, other_ref, ladder_ref = refs[count : count + 3]
    outs = refs[count + 3 : 2 * count + 3]
    rows_buf, cycle_buf, ladder_buf, sems, row_sems = refs[2 * count + 3 :]
    local_rows, depth = parts[0].shape
    slots, _, width = cycle_buf.shape
    blocks = own_ref.shape[1] // width
    q_part = depth // V
    j_part = ladder_ref.shape[0] // O

    def cycle_copy(half, b):
        at = pl.multiple_of(b * width, width)
        slot = lax.rem(half * blocks + b, slots)
        return pltpu.make_async_copy(
            (other_ref if half else own_ref).at[:, pl.ds(at, width)],
            cycle_buf.at[slot],
            sems.at[slot],
        )

    def start(b):
        @pl.when(b < blocks)
        def _():
            cycle_copy(0, b).start()

        @pl.when((b >= blocks) & (b < CORES * blocks))
        def _():
            cycle_copy(1, b - blocks).start()

    copies = [
        pltpu.make_async_copy(part, rows_buf.at[pl.ds(k * local_rows, local_rows)], row_sems.at[k])
        for k, part in enumerate(parts)
    ]
    for copy in copies:
        copy.start()
    for b in range(slots - 1):
        start(jnp.int32(b))
    for copy in copies:
        copy.wait()
    for n in range(count * local_rows // O):
        stacked = jnp.concatenate(
            [rows_buf[n * O : (n + 1) * O, q * V : (q + 1) * V] for q in range(q_part)], axis=0
        )
        term = jnp.dot(ladder_ref[...], stacked, preferred_element_type=jnp.float32)
        for j in range(j_part):
            ladder_buf[n * O : (n + 1) * O, j * V : (j + 1) * V] = term[j * O : (j + 1) * O]

    @pl.loop(0, CORES * blocks)
    def _(b):
        start(b + slots - 1)
        slot = lax.rem(b, slots)
        pltpu.make_async_copy(
            own_ref.at[:, pl.ds(0, width)], cycle_buf.at[slot], sems.at[slot]
        ).wait()
        columns = pl.ds(pl.multiple_of(b * width, width), width)
        value = jnp.dot(rows_buf[...], cycle_buf[slot], preferred_element_type=jnp.float32)
        value = value + ladder_buf[:, columns]
        for k in range(count):
            piece = value[k * local_rows : (k + 1) * local_rows]
            outs[k][:, columns] = encode(piece, PART_GAIN) if coded[k] else piece


def product(parts, cycle_block, other_block, ladder_rows, coded):
    local_rows, depth = parts[0].shape
    out_width = CORES * cycle_block.shape[1]
    width = 256 if cycle_block.shape[1] % 256 == 0 else V
    count = len(parts)
    rows = count * local_rows
    slots = 6
    hbm = pl.BlockSpec(memory_space=pl.ANY)
    vmem = pl.BlockSpec(memory_space=pltpu.VMEM)
    return pl.pallas_call(
        functools.partial(product_kernel, coded),
        in_specs=[hbm] * (count + 2) + [vmem],
        out_specs=[vmem] * count,
        out_shape=[
            jax.ShapeDtypeStruct((local_rows, out_width), jnp.bfloat16 if c else jnp.float32)
            for c in coded
        ],
        scratch_shapes=[
            pltpu.VMEM((rows, depth), jnp.bfloat16),
            pltpu.VMEM((slots, depth, width), jnp.bfloat16),
            pltpu.VMEM((rows, out_width), jnp.float32),
            pltpu.SemaphoreType.DMA((slots,)),
            pltpu.SemaphoreType.DMA((count,)),
        ],
        compiler_params=pltpu.CompilerParams(vmem_limit_bytes=48 * 1024 * 1024),
        cost_estimate=pl.CostEstimate(
            flops=2 * rows * out_width, bytes_accessed=2 * rows * out_width, transcendentals=0
        ),
    )(*parts, cycle_block, other_block, ladder_rows)


def power_of_two(exponent):
    return jnp.exp2(exponent).astype(jnp.bfloat16)


def after(value, *earlier):
    return lax.optimization_barrier((value,) + earlier)[0]


SUMS = 5


def sums_kernel(blocks, last, starts, occ, grow, rr, beta_prev, vir_ref, acc_in, r_ref, prev_ref, *refs):
    refs = refs[1:] if last else refs
    codes = refs[: blocks // CORES]
    sigma_ref, acc_ref, code_buf, r_buf, prev_buf, sigma_buf, sems = refs[blocks // CORES :]
    local_rows, row_width = r_ref.shape
    out_width = codes[0].shape[1] // CORES
    vectors = local_rows // O
    count_all = float(O * O * V)
    copies = []
    outward = []
    for b in range(blocks):
        columns = pl.ds(pl.multiple_of(starts[b], out_width), out_width)
        copies.append(
            [
                pltpu.make_async_copy(
                    codes[b // CORES].at[:, pl.ds(b % CORES * out_width, out_width)],
                    code_buf.at[b],
                    sems.at[0, b],
                ),
                pltpu.make_async_copy(r_ref.at[:, columns], r_buf.at[b], sems.at[1, b]),
                pltpu.make_async_copy(prev_ref.at[:, columns], prev_buf.at[b], sems.at[2, b]),
            ]
        )
        outward.append(
            pltpu.make_async_copy(sigma_buf.at[b], sigma_ref.at[:, columns], sems.at[3, b])
        )
    for group in copies:
        for copy in group:
            copy.start()
    occ_column = lax.broadcasted_iota(jnp.int32, (O, 1), 0)
    occ_rows = jnp.zeros((O, 1), jnp.float32)
    for i in range(O):
        occ_rows = jnp.where(occ_column == i, occ[i], occ_rows)
    base = vir_ref[...] - occ_rows
    acc_ref[...] = acc_in[...]

    def folded(value):
        return jnp.sum(value.reshape(O // 8, 8, V), axis=0)

    for b in range(blocks):
        for copy in copies[b]:
            copy.wait()

        @pl.loop(0, out_width // V)
        def _(j):
            columns = pl.ds(pl.multiple_of(j * V, V), V)
            level = base - occ[starts[b] // V + j]
            for v in range(vectors):
                rows = pl.ds(v * O, O)
                r = r_buf[b, rows, columns].astype(jnp.float32)
                p = prev_buf[b, rows, columns].astype(jnp.float32)
                value = decode(code_buf[b, rows, columns], SUM_GAIN) * grow[v] + level * r
                sigma_buf[b, rows, columns] = value
                for k, term in enumerate((value * value, value * r, value * p, r * p, p * p)):
                    acc_ref[SUMS * v + k] += folded(term)

        outward[b].start()
    if last:
        for v in range(vectors):
            ss, rs, sp, rp, pp = [
                jnp.full((1, 128), jnp.sum(acc_ref[SUMS * v + k])) for k in range(SUMS)
            ]
            beta = beta_prev[v]
            alpha = rs / count_all / (rr[v] / count_all + 1e-06)
            norm = (
                ss
                - 2.0 * alpha * rs
                - 2.0 * beta * sp
                + alpha * alpha * rr[v]
                + 2.0 * alpha * beta * rp
                + beta * beta * pp
            )
            acc_ref[SUMS * v, 0:1, 0:128] = alpha
            acc_ref[SUMS * v, 1:2, 0:128] = jnp.sqrt(norm / count_all + 1e-06)
    for copy in outward:
        copy.wait()


def add_sums(codes, starts, last, scalars, vir_row, acc, sigma, r_vector, r_previous):
    local_rows, row_width = r_vector.shape
    blocks = CORES * len(codes)
    out_width = codes[0].shape[1] // CORES
    smem = pl.BlockSpec(memory_space=pltpu.SMEM)
    hbm = pl.BlockSpec(memory_space=pl.ANY)
    vmem = pl.BlockSpec(memory_space=pltpu.VMEM)
    work = blocks * local_rows * out_width
    held = [sigma] if last else []
    return pl.pallas_call(
        functools.partial(sums_kernel, blocks, last),
        in_specs=[smem] * 5 + [vmem] * 2 + [hbm] * (2 + len(held) + len(codes)),
        out_specs=(hbm, vmem),
        out_shape=(
            jax.ShapeDtypeStruct((local_rows, row_width), jnp.float32),
            jax.ShapeDtypeStruct(acc.shape, jnp.float32),
        ),
        scratch_shapes=[
            pltpu.VMEM((blocks, local_rows, out_width), jnp.bfloat16),
            pltpu.VMEM((blocks, local_rows, out_width), jnp.bfloat16),
            pltpu.VMEM((blocks, local_rows, out_width), jnp.bfloat16),
            pltpu.VMEM((blocks, local_rows, out_width), jnp.float32),
            pltpu.SemaphoreType.DMA((4, blocks)),
        ],
        input_output_aliases={9: 0} if last else {},
        compiler_params=pltpu.CompilerParams(vmem_limit_bytes=58 * 1024 * 1024),
        cost_estimate=pl.CostEstimate(
            flops=30 * work, bytes_accessed=10 * work, transcendentals=2 * work
        ),
    )(starts, *scalars, vir_row, acc, r_vector, r_previous, *held, *codes)


def next_kernel(beta_prev, acc_ref, sigma_ref, r_ref, prev_ref, out_ref):
    for v in range(r_ref.shape[0] // O):
        rows = pl.ds(v * O, O)
        alpha = acc_ref[SUMS * v, 0:1, 0:1]
        scale = 1.0 / acc_ref[SUMS * v, 1:2, 0:1]
        value = (
            sigma_ref[rows, :]
            - alpha * r_ref[rows, :].astype(jnp.float32)
            - beta_prev[v] * prev_ref[rows, :].astype(jnp.float32)
        )
        out_ref[rows, :] = (value * scale).astype(out_ref.dtype)


def next_rows(beta_here, acc, sigma, r_vector, r_previous, width):
    local_rows, row_width = r_vector.shape
    block = pl.BlockSpec((local_rows, width), lambda i: (0, i))
    return pl.pallas_call(
        next_kernel,
        grid=(row_width // width,),
        in_specs=[
            pl.BlockSpec(memory_space=pltpu.SMEM),
            pl.BlockSpec(acc.shape, lambda i: (0, 0, 0)),
            block,
            block,
            block,
        ],
        out_specs=block,
        out_shape=jax.ShapeDtypeStruct((local_rows, row_width), jnp.bfloat16),
        compiler_params=pltpu.CompilerParams(vmem_limit_bytes=58 * 1024 * 1024),
        cost_estimate=pl.CostEstimate(
            flops=6 * local_rows * row_width,
            bytes_accessed=10 * local_rows * row_width,
            transcendentals=0,
        ),
    )(beta_here, acc, sigma, r_vector, r_previous)


def streamed(
    r_vector, r_previous, cycle_block, ladder_block, occ_energy, vir_energy, beta_previous
):
    n_row = lax.axis_size("row")
    n_col = lax.axis_size("col")
    n_chip = n_col // CORES
    local_rows, row_width = r_vector.shape
    vectors = local_rows // O
    depth = row_width // n_row
    out_width = cycle_block.shape[1]
    j_part = ladder_block.shape[1]
    q_part = ladder_block.shape[3]
    row_at = lax.axis_index("row")
    col_at = lax.axis_index("col")
    chip_at = col_at // CORES
    core_at = col_at % CORES
    order = list(range(0, n_chip, 2)) + list(range(1, n_chip, 2))[::-1]
    place = [order.index(chip) for chip in range(n_chip)]
    paired = n_row & (n_row - 1) == 0

    def partner(row, m):
        return row ^ m if paired else (row + m) % n_row

    def back(row, m):
        return row ^ m if paired else (row + n_row - m) % n_row

    def send(value, rows=0, hops=0, swap=0, reverse=False, route=None):
        pairs = []
        for row in range(n_row):
            for chip in range(n_chip):
                for core in range(CORES):
                    to_row = back(row, rows) if reverse else partner(row, rows)
                    to_chip = route[chip] if route else order[(place[chip] + hops) % n_chip]
                    to_core = (core + swap) % CORES
                    pairs.append(
                        (
                            row * n_col + chip * CORES + core,
                            to_row * n_col + to_chip * CORES + to_core,
                        )
                    )
        return lax.ppermute(value, AXES, pairs)

    other_block = send(cycle_block, swap=1)
    r_float = r_vector.astype(jnp.float32)
    rr_sum = jnp.sum(r_float.reshape(vectors, O * row_width) ** 2, axis=1)
    exponent = jnp.clip(jnp.floor(0.5 * jnp.log2(jnp.maximum(rr_sum, 1e-37))), -60.0, 60.0)
    shrink = jnp.repeat(power_of_two(-exponent), O)
    grow = power_of_two(exponent).astype(jnp.float32)

    def own_part(m):
        at = partner(row_at, m) * depth
        return lax.dynamic_slice_in_dim(r_vector, at, depth, axis=1) * shrink[:, None]

    mine = {(0, 0): own_part(0)}
    for m in range(1, n_row):
        part = own_part(m)
        if m == n_row - 1 and m > 2:
            part = after(part, mine[0, 1], mine[0, 2])
        mine[0, m] = send(part, rows=m)
    ladder_rows = after(ladder_block, mine[0, 1]).transpose(1, 0, 3, 2).reshape(j_part * O, q_part * O)
    ladder_rows = jnp.concatenate([ladder_rows, send(ladder_rows, swap=1)], axis=0)
    turns = []
    for s in range(n_chip):
        if s < 2:
            turn = list(range(n_row))
        else:
            turn = list(range(1, n_row)) + [0]
        turns += [(s, m) for m in turn]
    owner_sends = []
    for chip in range(n_chip):
        before = order[(place[chip] + n_chip - 1) % n_chip]
        owner = order[(place[chip] + 1) % n_chip]
        owner_sends.append((owner, chip, True) if abs(owner - chip) < abs(before - chip) else (before, chip, False))
    nearest = n_chip > 2 and len({source for source, _, _ in owner_sends}) == n_chip
    route = {source: chip for source, chip, _ in owner_sends}
    as_owner = jnp.array(
        [own for source in range(n_chip) for at, _, own in owner_sends if at == source][:n_chip]
        if nearest
        else [False] * n_chip
    )[chip_at]
    def pass_on(g, *earlier):
        s, m = turns[g]
        part = mine[s - 1, m]
        if s == n_chip - 1 and nearest:
            part = jnp.where(as_owner, mine[0, m], part)
        if g - 3 >= n_row:
            earlier += (mine[turns[g - 3]],)
        if earlier:
            part = after(part, *earlier)
        if s == n_chip - 1 and nearest:
            mine[s, m] = send(part, route=route)
        else:
            mine[s, m] = send(part, hops=1)

    order_table = jnp.array(order, dtype=jnp.int32)
    place_at = jnp.array(place, dtype=jnp.int32)[chip_at]
    starts = []
    for s in range(n_chip):
        for swap in range(CORES):
            chip = order_table[(place_at + s) % n_chip]
            starts.append((chip * CORES + (core_at + swap) % CORES) * out_width)
    starts = jnp.stack(starts)
    linear_index = row_at * n_col + col_at
    beta_here = lax.dynamic_slice_in_dim(beta_previous, linear_index * vectors, vectors)
    scalars = (occ_energy, grow, rr_sum, beta_here)

    groups = []
    for s in range(n_chip):
        turn = [(s, m) for m in list(range(1, n_row)) + [0]]
        if s < n_chip - 1:
            groups += [turn[k : k + 2] for k in range(0, n_row, 2)]
        else:
            groups += [turn[:2]] + [[at] for at in turn[2:]]
    last_of = {group[0][0]: g for g, group in enumerate(groups)}
    parts = {}
    arrived = {}
    codes = {}

    def summed(s):
        total = parts[s, 0]
        for k in range(1, n_row):
            total = total + decode(arrived[s, k], PART_GAIN)
        return encode(total, SUM_GAIN)

    sent = n_row
    while sent < min(2 * n_row, len(turns)):
        pass_on(sent, *([other_block] if sent == 2 * n_row - 1 else []))
        sent += 1
    acc = jnp.zeros((vectors * SUMS, 8, V), jnp.float32)
    vir_row = vir_energy[None, :]
    start_early, start_late = starts[: CORES * (n_chip - 1)], starts[CORES * (n_chip - 1) :]
    for g, group in enumerate(groups):
        s = group[0][0]
        earlier = []
        if g > 0:
            earlier.append(parts[groups[g - 1][0]])
        if g > 1:
            earlier += [arrived[at] for at in groups[g - 2] if at in arrived]
        for k in range(n_chip - 1):
            if last_of[k] + (2 if k < n_chip - 2 else 1) == g:
                code = summed(k)
                earlier.append(code)
                codes[k] = send(code, hops=n_chip - k) if k > 0 else code
        if n_row + g + 1 < sent and 0 < g <= n_row:
            earlier.append(mine[turns[n_row + g + 1]])
        for k in range(1, n_chip - 1):
            if k in codes and k < n_chip - 2 and g == last_of[k] + 4:
                earlier.append(codes[k])
        while any(at not in mine for at in group):
            pass_on(sent)
            sent += 1
        pieces = [mine[at] for at in group]
        if g == 0:
            pieces[0], start_early, start_late, vir_row, acc, *scalars = lax.optimization_barrier(
                (pieces[0], start_early, start_late, vir_row, acc, *scalars)
            )
        if earlier:
            pieces[0] = after(pieces[0], *earlier)
        made = product(pieces, cycle_block, other_block, ladder_rows, [m != 0 for _, m in group])
        for at, part in zip(group, made):
            parts[at] = part
            if at[1] != 0:
                arrived[at] = send(part, rows=at[1], reverse=True)
        if sent < len(turns):
            pass_on(sent, made[0])
            sent += 1
        if sent < len(turns) and g >= len(groups) - n_row - 1:
            pass_on(sent)
            sent += 1
    s = n_chip - 1
    if n_chip > 2:
        parts[s, 0] = after(parts[s, 0], codes[n_chip - 2])
    code = summed(s)
    codes[s] = send(code, hops=n_chip - s)
    early = [codes[k] for k in range(n_chip - 1)]
    late = [codes[s]]
    early[0] = after(early[0], code)
    sigma, acc = add_sums(
        early, start_early, False, scalars, vir_row, acc, None, r_vector, r_previous
    )
    sigma, acc = add_sums(
        late, start_late, True, scalars, vir_row, acc, sigma, r_vector, r_previous
    )
    next_vector = next_rows(beta_here, acc, sigma, r_vector, r_previous, out_width)
    both = acc.reshape(vectors, SUMS, 8, V)[:, 0, :2, 0].T
    whole = lax.dynamic_update_slice(
        jnp.zeros((2, NVEC), jnp.float32), both, (0, linear_index * vectors)
    )
    whole = whole + send(whole, swap=1)
    for group in ([{"hops": h} for h in range(1, n_chip)], [{"rows": m} for m in range(1, n_row)]):
        whole = sum([send(whole, **kind) for kind in group], whole)
    return (next_vector, whole[0], whole[1])


def gathered(
    r_vector, r_previous, cycle_block, ladder_block, occ_energy, vir_energy, beta_previous
):
    n_row = lax.axis_size("row")
    n_col = lax.axis_size("col")
    local_rows = r_vector.shape[0]
    row_width = r_vector.shape[1]
    all_rows = NVEC * O
    j_part = ladder_block.shape[1]
    q_part = ladder_block.shape[3]
    column_part = lax.all_to_all(r_vector, "row", split_axis=1, concat_axis=0, tiled=True)
    shaped = column_part.reshape(n_row, 1, local_rows, column_part.shape[1])
    gathered = lax.all_gather(shaped, "col", axis=1, tiled=True)
    operand = gathered.reshape(all_rows, column_part.shape[1])
    cycle_part = jnp.dot(operand, cycle_block, preferred_element_type=jnp.float32)
    ladder_part = jnp.einsum(
        "ijpq,npqa->nija",
        ladder_block,
        operand.reshape(NVEC, O, q_part, V),
        preferred_element_type=jnp.float32,
    )
    out_width = j_part * V
    partial_value = cycle_part + ladder_part.reshape(all_rows, out_width)
    summed = lax.psum_scatter(
        partial_value.reshape(n_row, n_col, local_rows, out_width),
        "row",
        scatter_dimension=0,
        tiled=True,
    )
    sigma_rows = lax.all_to_all(summed, "col", split_axis=1, concat_axis=3, tiled=True)
    sigma_rows = sigma_rows.reshape(local_rows, row_width)
    linear_index = lax.axis_index("row") * n_col + lax.axis_index("col")
    row_ids = linear_index * local_rows + jnp.arange(local_rows, dtype=jnp.int32)
    occ_index = row_ids % O
    vec_of_row = row_ids // O
    occ_rows = jnp.sum(
        jnp.where(occ_index[:, None] == jnp.arange(O)[None, :], occ_energy[None, :], 0.0), axis=1
    )
    r_float = r_vector.astype(jnp.float32)
    prev_float = r_previous.astype(jnp.float32)
    diagonal = vir_energy[None, None, :] - occ_rows[:, None, None] - occ_energy[None, :, None]
    sigma_rows = sigma_rows + (diagonal * r_float.reshape(local_rows, O, V)).reshape(
        local_rows, row_width
    )
    member = (vec_of_row[:, None] == jnp.arange(NVEC)[None, :]).astype(jnp.float32)
    count_all = O * O * V

    def per_vector(row_sums):
        return jnp.sum(member * row_sums[:, None], axis=0)

    def per_row(coefs):
        return jnp.sum(member * coefs[None, :], axis=1)

    ss_sum, rs_sum, rr_sum, sp_sum, rp_sum, pp_sum = lax.psum(
        (
            per_vector(jnp.sum(sigma_rows * sigma_rows, axis=1)),
            per_vector(jnp.sum(r_float * sigma_rows, axis=1)),
            per_vector(jnp.sum(r_float * r_float, axis=1)),
            per_vector(jnp.sum(prev_float * sigma_rows, axis=1)),
            per_vector(jnp.sum(r_float * prev_float, axis=1)),
            per_vector(jnp.sum(prev_float * prev_float, axis=1)),
        ),
        AXES,
    )
    alpha_coef = rs_sum / count_all / (rr_sum / count_all + 1e-06)
    norm_sum = (
        ss_sum
        - 2.0 * alpha_coef * rs_sum
        - 2.0 * beta_previous * sp_sum
        + alpha_coef * alpha_coef * rr_sum
        + 2.0 * alpha_coef * beta_previous * rp_sum
        + beta_previous * beta_previous * pp_sum
    )
    residual_vec = (
        sigma_rows
        - per_row(alpha_coef)[:, None] * r_float
        - per_row(beta_previous)[:, None] * prev_float
    )
    beta_coef = jnp.sqrt(norm_sum / count_all + 1e-06)
    next_vector = (residual_vec / per_row(beta_coef)[:, None]).astype(jnp.bfloat16)
    return (next_vector, alpha_coef, beta_coef)


def on_device(r_vector, *others):
    whole_vectors = r_vector.shape[0] % O == 0 and lax.axis_size("col") % CORES == 0
    body = streamed if whole_vectors else gathered
    return body(r_vector, *others)


def solution(mesh):
    placed = (
        P(AXES, None),
        P(AXES, None),
        P("row", "col"),
        P(None, "col", None, "row"),
        P(),
        P(),
        P(),
    )
    return jax.shard_map(
        on_device,
        mesh=mesh,
        in_specs=placed,
        out_specs=(P(AXES, None), P(), P()),
        check_vma=False,
    )
```

```python
import functools

import jax
import jax.numpy as jnp
from jax import lax
from jax.experimental import pallas as pl
from jax.experimental.pallas import tpu as pltpu
from jax.sharding import PartitionSpec as P

O = 48
V = 384
NVEC = 64
CORES = 2
AXES = ("row", "col")
POWER = 16
FLOOR = 2.0**-7.75
PART_GAIN = 16.0
SUM_GAIN = 8.0


def encode(value, gain):
    size = jnp.abs(value) * gain + FLOOR
    size = size * size
    size = size * size
    size = size * size
    size = size * size
    return jnp.where(value < 0, -size, size).astype(jnp.bfloat16)


def decode(code, gain):
    wide = code.astype(jnp.float32)
    size = (jnp.exp2(jnp.log2(jnp.abs(wide)) * (1.0 / POWER)) - FLOOR) * (1.0 / gain)
    return jnp.where(wide < 0, -size, size)


def product_kernel(coded, *refs):
    count = len(coded)
    parts = refs[:count]
    own_ref, other_ref, ladder_ref = refs[count : count + 3]
    outs = refs[count + 3 : 2 * count + 3]
    rows_buf, cycle_buf, ladder_buf, sems, row_sems = refs[2 * count + 3 :]
    local_rows, depth = parts[0].shape
    slots, _, width = cycle_buf.shape
    blocks = own_ref.shape[1] // width
    q_part = depth // V
    j_part = ladder_ref.shape[0] // O

    def cycle_copy(half, b):
        at = pl.multiple_of(b * width, width)
        slot = lax.rem(half * blocks + b, slots)
        return pltpu.make_async_copy(
            (other_ref if half else own_ref).at[:, pl.ds(at, width)],
            cycle_buf.at[slot],
            sems.at[slot],
        )

    def start(b):
        @pl.when(b < blocks)
        def _():
            cycle_copy(0, b).start()

        @pl.when((b >= blocks) & (b < CORES * blocks))
        def _():
            cycle_copy(1, b - blocks).start()

    copies = [
        pltpu.make_async_copy(part, rows_buf.at[pl.ds(k * local_rows, local_rows)], row_sems.at[k])
        for k, part in enumerate(parts)
    ]
    for copy in copies:
        copy.start()
    for b in range(slots - 1):
        start(jnp.int32(b))
    for copy in copies:
        copy.wait()
    for n in range(count * local_rows // O):
        stacked = jnp.concatenate(
            [rows_buf[n * O : (n + 1) * O, q * V : (q + 1) * V] for q in range(q_part)], axis=0
        )
        term = jnp.dot(ladder_ref[...], stacked, preferred_element_type=jnp.float32)
        for j in range(j_part):
            ladder_buf[n * O : (n + 1) * O, j * V : (j + 1) * V] = term[j * O : (j + 1) * O]

    @pl.loop(0, CORES * blocks)
    def _(b):
        start(b + slots - 1)
        slot = lax.rem(b, slots)
        pltpu.make_async_copy(
            own_ref.at[:, pl.ds(0, width)], cycle_buf.at[slot], sems.at[slot]
        ).wait()
        columns = pl.ds(pl.multiple_of(b * width, width), width)
        value = jnp.dot(rows_buf[...], cycle_buf[slot], preferred_element_type=jnp.float32)
        value = value + ladder_buf[:, columns]
        for k in range(count):
            piece = value[k * local_rows : (k + 1) * local_rows]
            outs[k][:, columns] = encode(piece, PART_GAIN) if coded[k] else piece


def product(parts, cycle_block, other_block, ladder_rows, coded):
    local_rows, depth = parts[0].shape
    out_width = CORES * cycle_block.shape[1]
    width = 256 if cycle_block.shape[1] % 256 == 0 else V
    count = len(parts)
    rows = count * local_rows
    slots = 6
    hbm = pl.BlockSpec(memory_space=pl.ANY)
    vmem = pl.BlockSpec(memory_space=pltpu.VMEM)
    return pl.pallas_call(
        functools.partial(product_kernel, coded),
        in_specs=[hbm] * (count + 2) + [vmem],
        out_specs=[vmem] * count,
        out_shape=[
            jax.ShapeDtypeStruct((local_rows, out_width), jnp.bfloat16 if c else jnp.float32)
            for c in coded
        ],
        scratch_shapes=[
            pltpu.VMEM((rows, depth), jnp.bfloat16),
            pltpu.VMEM((slots, depth, width), jnp.bfloat16),
            pltpu.VMEM((rows, out_width), jnp.float32),
            pltpu.SemaphoreType.DMA((slots,)),
            pltpu.SemaphoreType.DMA((count,)),
        ],
        compiler_params=pltpu.CompilerParams(vmem_limit_bytes=48 * 1024 * 1024),
        cost_estimate=pl.CostEstimate(
            flops=2 * rows * out_width, bytes_accessed=2 * rows * out_width, transcendentals=0
        ),
    )(*parts, cycle_block, other_block, ladder_rows)


def power_of_two(exponent):
    return jnp.exp2(exponent).astype(jnp.bfloat16)


def after(value, *earlier):
    return lax.optimization_barrier((value,) + earlier)[0]


SUMS = 3


def sums_kernel(blocks, last, starts, occ, grow, rr, beta_prev, vir_ref, acc_in, r_ref, prev_ref, *refs):
    refs = refs[1:] if last else refs
    codes = refs[: blocks // CORES]
    rest_ref, acc_ref, code_buf, r_buf, prev_buf, rest_buf, sems = refs[blocks // CORES :]
    local_rows, row_width = r_ref.shape
    out_width = codes[0].shape[1] // CORES
    vectors = local_rows // O
    count_all = float(O * O * V)
    copies = []
    outward = []
    for b in range(blocks):
        columns = pl.ds(pl.multiple_of(starts[b], out_width), out_width)
        copies.append(
            [
                pltpu.make_async_copy(
                    codes[b // CORES].at[:, pl.ds(b % CORES * out_width, out_width)],
                    code_buf.at[b],
                    sems.at[0, b],
                ),
                pltpu.make_async_copy(r_ref.at[:, columns], r_buf.at[b], sems.at[1, b]),
                pltpu.make_async_copy(prev_ref.at[:, columns], prev_buf.at[b], sems.at[2, b]),
            ]
        )
        outward.append(
            pltpu.make_async_copy(rest_buf.at[b], rest_ref.at[:, columns], sems.at[3, b])
        )
    for group in copies:
        for copy in group:
            copy.start()
    occ_column = lax.broadcasted_iota(jnp.int32, (O, 1), 0)
    occ_rows = jnp.zeros((O, 1), jnp.float32)
    for i in range(O):
        occ_rows = jnp.where(occ_column == i, occ[i], occ_rows)
    base = vir_ref[...] - occ_rows
    acc_ref[...] = acc_in[...]

    def folded(value):
        return jnp.sum(value.reshape(O // 8, 8, V), axis=0)

    for b in range(blocks):
        for copy in copies[b]:
            copy.wait()

        @pl.loop(0, out_width // V)
        def _(j):
            columns = pl.ds(pl.multiple_of(j * V, V), V)
            level = base - occ[starts[b] // V + j]
            for v in range(vectors):
                rows = pl.ds(v * O, O)
                r = r_buf[b, rows, columns].astype(jnp.float32)
                p = prev_buf[b, rows, columns].astype(jnp.float32)
                value = decode(code_buf[b, rows, columns], SUM_GAIN) * grow[v] + level * r
                rest = value - beta_prev[v] * p
                rest_buf[b, rows, columns] = rest
                for k, term in enumerate((rest * rest, value * r, rest * r)):
                    acc_ref[SUMS * v + k] += folded(term)

        outward[b].start()
    if last:
        for v in range(vectors):
            tt, rs, tr = [
                jnp.full((1, 128), jnp.sum(acc_ref[SUMS * v + k])) for k in range(SUMS)
            ]
            alpha = rs / count_all / (rr[v] / count_all + 1e-06)
            norm = tt - 2.0 * alpha * tr + alpha * alpha * rr[v]
            acc_ref[SUMS * v, 0:1, 0:128] = alpha
            acc_ref[SUMS * v, 1:2, 0:128] = jnp.sqrt(norm / count_all + 1e-06)
    for copy in outward:
        copy.wait()


def add_sums(codes, starts, last, scalars, vir_row, acc, rest, r_vector, r_previous):
    local_rows, row_width = r_vector.shape
    blocks = CORES * len(codes)
    out_width = codes[0].shape[1] // CORES
    smem = pl.BlockSpec(memory_space=pltpu.SMEM)
    hbm = pl.BlockSpec(memory_space=pl.ANY)
    vmem = pl.BlockSpec(memory_space=pltpu.VMEM)
    work = blocks * local_rows * out_width
    held = [rest] if last else []
    return pl.pallas_call(
        functools.partial(sums_kernel, blocks, last),
        in_specs=[smem] * 5 + [vmem] * 2 + [hbm] * (2 + len(held) + len(codes)),
        out_specs=(hbm, vmem),
        out_shape=(
            jax.ShapeDtypeStruct((local_rows, row_width), jnp.float32),
            jax.ShapeDtypeStruct(acc.shape, jnp.float32),
        ),
        scratch_shapes=[
            pltpu.VMEM((blocks, local_rows, out_width), jnp.bfloat16),
            pltpu.VMEM((blocks, local_rows, out_width), jnp.bfloat16),
            pltpu.VMEM((blocks, local_rows, out_width), jnp.bfloat16),
            pltpu.VMEM((blocks, local_rows, out_width), jnp.float32),
            pltpu.SemaphoreType.DMA((4, blocks)),
        ],
        input_output_aliases={9: 0} if last else {},
        compiler_params=pltpu.CompilerParams(vmem_limit_bytes=58 * 1024 * 1024),
        cost_estimate=pl.CostEstimate(
            flops=30 * work, bytes_accessed=10 * work, transcendentals=2 * work
        ),
    )(starts, *scalars, vir_row, acc, r_vector, r_previous, *held, *codes)


def next_kernel(acc_ref, rest_ref, r_ref, out_ref):
    for v in range(r_ref.shape[0] // O):
        rows = pl.ds(v * O, O)
        alpha = acc_ref[SUMS * v, 0:1, 0:1]
        scale = 1.0 / acc_ref[SUMS * v, 1:2, 0:1]
        value = rest_ref[rows, :] - alpha * r_ref[rows, :].astype(jnp.float32)
        out_ref[rows, :] = (value * scale).astype(out_ref.dtype)


def next_rows(acc, rest, r_vector, width):
    local_rows, row_width = r_vector.shape
    block = pl.BlockSpec((local_rows, width), lambda i: (0, i))
    return pl.pallas_call(
        next_kernel,
        grid=(row_width // width,),
        in_specs=[
            pl.BlockSpec(acc.shape, lambda i: (0, 0, 0)),
            block,
            block,
        ],
        out_specs=block,
        out_shape=jax.ShapeDtypeStruct((local_rows, row_width), jnp.bfloat16),
        compiler_params=pltpu.CompilerParams(vmem_limit_bytes=58 * 1024 * 1024),
        cost_estimate=pl.CostEstimate(
            flops=6 * local_rows * row_width,
            bytes_accessed=8 * local_rows * row_width,
            transcendentals=0,
        ),
    )(acc, rest, r_vector)


def streamed(
    r_vector, r_previous, cycle_block, ladder_block, occ_energy, vir_energy, beta_previous
):
    n_row = lax.axis_size("row")
    n_col = lax.axis_size("col")
    n_chip = n_col // CORES
    local_rows, row_width = r_vector.shape
    vectors = local_rows // O
    depth = row_width // n_row
    out_width = cycle_block.shape[1]
    j_part = ladder_block.shape[1]
    q_part = ladder_block.shape[3]
    row_at = lax.axis_index("row")
    col_at = lax.axis_index("col")
    chip_at = col_at // CORES
    core_at = col_at % CORES
    order = list(range(0, n_chip, 2)) + list(range(1, n_chip, 2))[::-1]
    place = [order.index(chip) for chip in range(n_chip)]
    paired = n_row & (n_row - 1) == 0

    def partner(row, m):
        return row ^ m if paired else (row + m) % n_row

    def back(row, m):
        return row ^ m if paired else (row + n_row - m) % n_row

    def send(value, rows=0, hops=0, swap=0, reverse=False, route=None):
        pairs = []
        for row in range(n_row):
            for chip in range(n_chip):
                for core in range(CORES):
                    to_row = back(row, rows) if reverse else partner(row, rows)
                    to_chip = route[chip] if route else order[(place[chip] + hops) % n_chip]
                    to_core = (core + swap) % CORES
                    pairs.append(
                        (
                            row * n_col + chip * CORES + core,
                            to_row * n_col + to_chip * CORES + to_core,
                        )
                    )
        return lax.ppermute(value, AXES, pairs)

    other_block = send(cycle_block, swap=1)
    r_float = r_vector.astype(jnp.float32)
    rr_sum = jnp.sum(r_float.reshape(vectors, O * row_width) ** 2, axis=1)
    exponent = jnp.clip(jnp.floor(0.5 * jnp.log2(jnp.maximum(rr_sum, 1e-37))), -60.0, 60.0)
    shrink = jnp.repeat(power_of_two(-exponent), O)
    grow = power_of_two(exponent).astype(jnp.float32)

    def own_part(m):
        at = partner(row_at, m) * depth
        return lax.dynamic_slice_in_dim(r_vector, at, depth, axis=1) * shrink[:, None]

    mine = {(0, 0): own_part(0)}
    for m in range(1, n_row):
        part = own_part(m)
        if m == n_row - 1 and m > 2:
            part = after(part, mine[0, 1], mine[0, 2])
        mine[0, m] = send(part, rows=m)
    ladder_rows = after(ladder_block, mine[0, 1]).transpose(1, 0, 3, 2).reshape(j_part * O, q_part * O)
    ladder_rows = jnp.concatenate([ladder_rows, send(ladder_rows, swap=1)], axis=0)
    turns = []
    for s in range(n_chip):
        if s < 2:
            turn = list(range(n_row))
        else:
            turn = list(range(1, n_row)) + [0]
        turns += [(s, m) for m in turn]
    owner_sends = []
    for chip in range(n_chip):
        before = order[(place[chip] + n_chip - 1) % n_chip]
        owner = order[(place[chip] + 1) % n_chip]
        owner_sends.append((owner, chip, True) if abs(owner - chip) < abs(before - chip) else (before, chip, False))
    nearest = n_chip > 2 and len({source for source, _, _ in owner_sends}) == n_chip
    route = {source: chip for source, chip, _ in owner_sends}
    as_owner = jnp.array(
        [own for source in range(n_chip) for at, _, own in owner_sends if at == source][:n_chip]
        if nearest
        else [False] * n_chip
    )[chip_at]
    def pass_on(g, *earlier):
        s, m = turns[g]
        part = mine[s - 1, m]
        if s == n_chip - 1 and nearest:
            part = jnp.where(as_owner, mine[0, m], part)
        lag = 2 if s == n_chip - 1 else 3
        if g - lag >= n_row:
            earlier += (mine[turns[g - lag]],)
        if earlier:
            part = after(part, *earlier)
        if s == n_chip - 1 and nearest:
            mine[s, m] = send(part, route=route)
        else:
            mine[s, m] = send(part, hops=1)

    order_table = jnp.array(order, dtype=jnp.int32)
    place_at = jnp.array(place, dtype=jnp.int32)[chip_at]
    starts = []
    for s in range(n_chip):
        for swap in range(CORES):
            chip = order_table[(place_at + s) % n_chip]
            starts.append((chip * CORES + (core_at + swap) % CORES) * out_width)
    starts = jnp.stack(starts)
    linear_index = row_at * n_col + col_at
    beta_here = lax.dynamic_slice_in_dim(beta_previous, linear_index * vectors, vectors)
    scalars = (occ_energy, grow, rr_sum, beta_here)

    groups = []
    for s in range(n_chip):
        turn = [(s, m) for m in list(range(1, n_row)) + [0]]
        if s < n_chip - 1:
            groups += [turn[k : k + 2] for k in range(0, n_row, 2)]
        else:
            groups += [turn[:2]] + [[at] for at in turn[2:]]
    last_of = {group[0][0]: g for g, group in enumerate(groups)}
    parts = {}
    arrived = {}
    codes = {}

    def summed(s):
        total = parts[s, 0]
        for k in range(1, n_row):
            total = total + decode(arrived[s, k], PART_GAIN)
        return encode(total, SUM_GAIN)

    sent = n_row
    while sent < min(2 * n_row, len(turns)):
        pass_on(sent, *([other_block] if sent == 2 * n_row - 1 else []))
        sent += 1
    acc = jnp.zeros((vectors * SUMS, 8, V), jnp.float32)
    vir_row = vir_energy[None, :]
    start_early, start_late = starts[: CORES * (n_chip - 1)], starts[CORES * (n_chip - 1) :]
    for g, group in enumerate(groups):
        s = group[0][0]
        earlier = []
        if g > 0:
            earlier.append(parts[groups[g - 1][0]])
        if g > 1:
            earlier += [arrived[at] for at in groups[g - 2] if at in arrived]
        for k in range(n_chip - 1):
            if last_of[k] + 2 == g:
                code = summed(k)
                earlier.append(code)
                codes[k] = send(code, hops=n_chip - k) if k > 0 else code
        if n_row + g + 1 < sent and 0 < g <= n_row:
            earlier.append(mine[turns[n_row + g + 1]])
        for k in range(1, n_chip - 1):
            if k in codes and k < n_chip - 2 and g == last_of[k] + 4:
                earlier.append(codes[k])
        while any(at not in mine for at in group):
            pass_on(sent)
            sent += 1
        pieces = [mine[at] for at in group]
        if g == 0:
            pieces[0], start_early, start_late, vir_row, acc, *scalars = lax.optimization_barrier(
                (pieces[0], start_early, start_late, vir_row, acc, *scalars)
            )
        if earlier:
            pieces[0] = after(pieces[0], *earlier)
        made = product(pieces, cycle_block, other_block, ladder_rows, [m != 0 for _, m in group])
        for at, part in zip(group, made):
            parts[at] = part
            if at[1] != 0:
                arrived[at] = send(part, rows=at[1], reverse=True)
        if sent < len(turns):
            pass_on(sent, made[0])
            sent += 1
        if sent < len(turns) and g >= len(groups) - n_row - 1:
            pass_on(sent)
            sent += 1
    s = n_chip - 1
    code = summed(s)
    codes[s] = send(after(code, codes[n_chip - 2]), hops=n_chip - s)
    early = [codes[k] for k in range(n_chip - 1)]
    late = [codes[s]]
    early[0] = after(early[0], code)
    rest, acc = add_sums(
        early, start_early, False, scalars, vir_row, acc, None, r_vector, r_previous
    )
    rest, acc = add_sums(
        late, start_late, True, scalars, vir_row, acc, rest, r_vector, r_previous
    )
    next_vector = next_rows(acc, rest, r_vector, out_width)
    both = acc.reshape(vectors, SUMS, 8, V)[:, 0, :2, 0].T
    whole = lax.dynamic_update_slice(
        jnp.zeros((2, NVEC), jnp.float32), both, (0, linear_index * vectors)
    )
    whole = whole + send(whole, swap=1)
    for group in ([{"hops": h} for h in range(1, n_chip)], [{"rows": m} for m in range(1, n_row)]):
        whole = sum([send(whole, **kind) for kind in group], whole)
    return (next_vector, whole[0], whole[1])


def gathered(
    r_vector, r_previous, cycle_block, ladder_block, occ_energy, vir_energy, beta_previous
):
    n_row = lax.axis_size("row")
    n_col = lax.axis_size("col")
    local_rows = r_vector.shape[0]
    row_width = r_vector.shape[1]
    all_rows = NVEC * O
    j_part = ladder_block.shape[1]
    q_part = ladder_block.shape[3]
    column_part = lax.all_to_all(r_vector, "row", split_axis=1, concat_axis=0, tiled=True)
    shaped = column_part.reshape(n_row, 1, local_rows, column_part.shape[1])
    gathered = lax.all_gather(shaped, "col", axis=1, tiled=True)
    operand = gathered.reshape(all_rows, column_part.shape[1])
    cycle_part = jnp.dot(operand, cycle_block, preferred_element_type=jnp.float32)
    ladder_part = jnp.einsum(
        "ijpq,npqa->nija",
        ladder_block,
        operand.reshape(NVEC, O, q_part, V),
        preferred_element_type=jnp.float32,
    )
    out_width = j_part * V
    partial_value = cycle_part + ladder_part.reshape(all_rows, out_width)
    summed = lax.psum_scatter(
        partial_value.reshape(n_row, n_col, local_rows, out_width),
        "row",
        scatter_dimension=0,
        tiled=True,
    )
    sigma_rows = lax.all_to_all(summed, "col", split_axis=1, concat_axis=3, tiled=True)
    sigma_rows = sigma_rows.reshape(local_rows, row_width)
    linear_index = lax.axis_index("row") * n_col + lax.axis_index("col")
    row_ids = linear_index * local_rows + jnp.arange(local_rows, dtype=jnp.int32)
    occ_index = row_ids % O
    vec_of_row = row_ids // O
    occ_rows = jnp.sum(
        jnp.where(occ_index[:, None] == jnp.arange(O)[None, :], occ_energy[None, :], 0.0), axis=1
    )
    r_float = r_vector.astype(jnp.float32)
    prev_float = r_previous.astype(jnp.float32)
    diagonal = vir_energy[None, None, :] - occ_rows[:, None, None] - occ_energy[None, :, None]
    sigma_rows = sigma_rows + (diagonal * r_float.reshape(local_rows, O, V)).reshape(
        local_rows, row_width
    )
    member = (vec_of_row[:, None] == jnp.arange(NVEC)[None, :]).astype(jnp.float32)
    count_all = O * O * V

    def per_vector(row_sums):
        return jnp.sum(member * row_sums[:, None], axis=0)

    def per_row(coefs):
        return jnp.sum(member * coefs[None, :], axis=1)

    ss_sum, rs_sum, rr_sum, sp_sum, rp_sum, pp_sum = lax.psum(
        (
            per_vector(jnp.sum(sigma_rows * sigma_rows, axis=1)),
            per_vector(jnp.sum(r_float * sigma_rows, axis=1)),
            per_vector(jnp.sum(r_float * r_float, axis=1)),
            per_vector(jnp.sum(prev_float * sigma_rows, axis=1)),
            per_vector(jnp.sum(r_float * prev_float, axis=1)),
            per_vector(jnp.sum(prev_float * prev_float, axis=1)),
        ),
        AXES,
    )
    alpha_coef = rs_sum / count_all / (rr_sum / count_all + 1e-06)
    norm_sum = (
        ss_sum
        - 2.0 * alpha_coef * rs_sum
        - 2.0 * beta_previous * sp_sum
        + alpha_coef * alpha_coef * rr_sum
        + 2.0 * alpha_coef * beta_previous * rp_sum
        + beta_previous * beta_previous * pp_sum
    )
    residual_vec = (
        sigma_rows
        - per_row(alpha_coef)[:, None] * r_float
        - per_row(beta_previous)[:, None] * prev_float
    )
    beta_coef = jnp.sqrt(norm_sum / count_all + 1e-06)
    next_vector = (residual_vec / per_row(beta_coef)[:, None]).astype(jnp.bfloat16)
    return (next_vector, alpha_coef, beta_coef)


def on_device(r_vector, *others):
    whole_vectors = r_vector.shape[0] % O == 0 and lax.axis_size("col") % CORES == 0
    body = streamed if whole_vectors else gathered
    return body(r_vector, *others)


def solution(mesh):
    placed = (
        P(AXES, None),
        P(AXES, None),
        P("row", "col"),
        P(None, "col", None, "row"),
        P(),
        P(),
        P(),
    )
    return jax.shard_map(
        on_device,
        mesh=mesh,
        in_specs=placed,
        out_specs=(P(AXES, None), P(), P()),
        check_vma=False,
    )
```

```python
import functools

import jax
import jax.numpy as jnp
from jax import lax
from jax.experimental import pallas as pl
from jax.experimental.pallas import tpu as pltpu
from jax.sharding import PartitionSpec as P

O = 48
V = 384
NVEC = 64
CORES = 2
AXES = ("row", "col")
POWER = 16
FLOOR = 2.0**-7.75
PART_GAIN = 16.0
SUM_GAIN = 8.0


def encode(value, gain):
    size = jnp.abs(value) * gain + FLOOR
    size = size * size
    size = size * size
    size = size * size
    size = size * size
    return jnp.where(value < 0, -size, size).astype(jnp.bfloat16)


def decode(code, gain):
    wide = code.astype(jnp.float32)
    size = (jnp.exp2(jnp.log2(jnp.abs(wide)) * (1.0 / POWER)) - FLOOR) * (1.0 / gain)
    return jnp.where(wide < 0, -size, size)


def product_kernel(coded, *refs):
    count = len(coded)
    parts = refs[:count]
    own_ref, other_ref, ladder_ref = refs[count : count + 3]
    outs = refs[count + 3 : 2 * count + 3]
    rows_buf, cycle_buf, ladder_buf, sems, row_sems = refs[2 * count + 3 :]
    local_rows, depth = parts[0].shape
    slots, _, width = cycle_buf.shape
    blocks = own_ref.shape[1] // width
    q_part = depth // V
    j_part = ladder_ref.shape[0] // O

    def cycle_copy(half, b):
        at = pl.multiple_of(b * width, width)
        slot = lax.rem(half * blocks + b, slots)
        return pltpu.make_async_copy(
            (other_ref if half else own_ref).at[:, pl.ds(at, width)],
            cycle_buf.at[slot],
            sems.at[slot],
        )

    def start(b):
        @pl.when(b < blocks)
        def _():
            cycle_copy(0, b).start()

        @pl.when((b >= blocks) & (b < CORES * blocks))
        def _():
            cycle_copy(1, b - blocks).start()

    copies = [
        pltpu.make_async_copy(part, rows_buf.at[pl.ds(k * local_rows, local_rows)], row_sems.at[k])
        for k, part in enumerate(parts)
    ]
    for copy in copies:
        copy.start()
    for b in range(slots - 1):
        start(jnp.int32(b))
    for copy in copies:
        copy.wait()
    for n in range(count * local_rows // O):
        stacked = jnp.concatenate(
            [rows_buf[n * O : (n + 1) * O, q * V : (q + 1) * V] for q in range(q_part)], axis=0
        )
        term = jnp.dot(ladder_ref[...], stacked, preferred_element_type=jnp.float32)
        for j in range(j_part):
            ladder_buf[n * O : (n + 1) * O, j * V : (j + 1) * V] = term[j * O : (j + 1) * O]

    @pl.loop(0, CORES * blocks)
    def _(b):
        start(b + slots - 1)
        slot = lax.rem(b, slots)
        pltpu.make_async_copy(
            own_ref.at[:, pl.ds(0, width)], cycle_buf.at[slot], sems.at[slot]
        ).wait()
        columns = pl.ds(pl.multiple_of(b * width, width), width)
        value = jnp.dot(rows_buf[...], cycle_buf[slot], preferred_element_type=jnp.float32)
        value = value + ladder_buf[:, columns]
        for k in range(count):
            piece = value[k * local_rows : (k + 1) * local_rows]
            outs[k][:, columns] = encode(piece, PART_GAIN) if coded[k] else piece


def product(parts, cycle_block, other_block, ladder_rows, coded):
    local_rows, depth = parts[0].shape
    out_width = CORES * cycle_block.shape[1]
    width = 256 if cycle_block.shape[1] % 256 == 0 else V
    count = len(parts)
    rows = count * local_rows
    slots = 6
    hbm = pl.BlockSpec(memory_space=pl.ANY)
    vmem = pl.BlockSpec(memory_space=pltpu.VMEM)
    return pl.pallas_call(
        functools.partial(product_kernel, coded),
        in_specs=[hbm] * (count + 2) + [vmem],
        out_specs=[vmem] * count,
        out_shape=[
            jax.ShapeDtypeStruct((local_rows, out_width), jnp.bfloat16 if c else jnp.float32)
            for c in coded
        ],
        scratch_shapes=[
            pltpu.VMEM((rows, depth), jnp.bfloat16),
            pltpu.VMEM((slots, depth, width), jnp.bfloat16),
            pltpu.VMEM((rows, out_width), jnp.float32),
            pltpu.SemaphoreType.DMA((slots,)),
            pltpu.SemaphoreType.DMA((count,)),
        ],
        compiler_params=pltpu.CompilerParams(vmem_limit_bytes=48 * 1024 * 1024),
        cost_estimate=pl.CostEstimate(
            flops=2 * rows * out_width, bytes_accessed=2 * rows * out_width, transcendentals=0
        ),
    )(*parts, cycle_block, other_block, ladder_rows)


def power_of_two(exponent):
    return jnp.exp2(exponent).astype(jnp.bfloat16)


def after(value, *earlier):
    return lax.optimization_barrier((value,) + earlier)[0]


SUMS = 3


def sums_kernel(blocks, last, starts, occ, grow, rr, beta_prev, vir_ref, acc_in, r_ref, prev_ref, *refs):
    refs = refs[1:] if last else refs
    codes = refs[: blocks // CORES]
    rest_ref, acc_ref, code_buf, r_buf, prev_buf, rest_buf, sems = refs[blocks // CORES :]
    local_rows, row_width = r_ref.shape
    out_width = codes[0].shape[1] // CORES
    vectors = local_rows // O
    count_all = float(O * O * V)
    copies = []
    outward = []
    for b in range(blocks):
        columns = pl.ds(pl.multiple_of(starts[b], out_width), out_width)
        copies.append(
            [
                pltpu.make_async_copy(
                    codes[b // CORES].at[:, pl.ds(b % CORES * out_width, out_width)],
                    code_buf.at[b],
                    sems.at[0, b],
                ),
                pltpu.make_async_copy(r_ref.at[:, columns], r_buf.at[b], sems.at[1, b]),
                pltpu.make_async_copy(prev_ref.at[:, columns], prev_buf.at[b], sems.at[2, b]),
            ]
        )
        outward.append(
            pltpu.make_async_copy(rest_buf.at[b], rest_ref.at[:, columns], sems.at[3, b])
        )
    for group in copies:
        for copy in group:
            copy.start()
    occ_column = lax.broadcasted_iota(jnp.int32, (O, 1), 0)
    occ_rows = jnp.zeros((O, 1), jnp.float32)
    for i in range(O):
        occ_rows = jnp.where(occ_column == i, occ[i], occ_rows)
    base = vir_ref[...] - occ_rows
    acc_ref[...] = acc_in[...]

    def folded(value):
        return jnp.sum(value.reshape(O // 8, 8, V), axis=0)

    for b in range(blocks):
        for copy in copies[b]:
            copy.wait()

        @pl.loop(0, out_width // V)
        def _(j):
            columns = pl.ds(pl.multiple_of(j * V, V), V)
            level = base - occ[starts[b] // V + j]
            for v in range(vectors):
                rows = pl.ds(v * O, O)
                r = r_buf[b, rows, columns].astype(jnp.float32)
                p = prev_buf[b, rows, columns].astype(jnp.float32)
                value = decode(code_buf[b, rows, columns], SUM_GAIN) * grow[v] + level * r
                rest = value - beta_prev[v] * p
                rest_buf[b, rows, columns] = rest
                for k, term in enumerate((rest * rest, value * r, rest * r)):
                    acc_ref[SUMS * v + k] += folded(term)

        outward[b].start()
    if last:
        for v in range(vectors):
            tt, rs, tr = [
                jnp.full((1, 128), jnp.sum(acc_ref[SUMS * v + k])) for k in range(SUMS)
            ]
            alpha = rs / count_all / (rr[v] / count_all + 1e-06)
            norm = tt - 2.0 * alpha * tr + alpha * alpha * rr[v]
            acc_ref[SUMS * v, 0:1, 0:128] = alpha
            acc_ref[SUMS * v, 1:2, 0:128] = jnp.sqrt(norm / count_all + 1e-06)
    for copy in outward:
        copy.wait()


def add_sums(codes, starts, last, scalars, vir_row, acc, rest, r_vector, r_previous):
    local_rows, row_width = r_vector.shape
    blocks = CORES * len(codes)
    out_width = codes[0].shape[1] // CORES
    smem = pl.BlockSpec(memory_space=pltpu.SMEM)
    hbm = pl.BlockSpec(memory_space=pl.ANY)
    vmem = pl.BlockSpec(memory_space=pltpu.VMEM)
    work = blocks * local_rows * out_width
    held = [rest] if last else []
    return pl.pallas_call(
        functools.partial(sums_kernel, blocks, last),
        in_specs=[smem] * 5 + [vmem] * 2 + [hbm] * (2 + len(held) + len(codes)),
        out_specs=(hbm, vmem),
        out_shape=(
            jax.ShapeDtypeStruct((local_rows, row_width), jnp.float32),
            jax.ShapeDtypeStruct(acc.shape, jnp.float32),
        ),
        scratch_shapes=[
            pltpu.VMEM((blocks, local_rows, out_width), jnp.bfloat16),
            pltpu.VMEM((blocks, local_rows, out_width), jnp.bfloat16),
            pltpu.VMEM((blocks, local_rows, out_width), jnp.bfloat16),
            pltpu.VMEM((blocks, local_rows, out_width), jnp.float32),
            pltpu.SemaphoreType.DMA((4, blocks)),
        ],
        input_output_aliases={9: 0} if last else {},
        compiler_params=pltpu.CompilerParams(vmem_limit_bytes=58 * 1024 * 1024),
        cost_estimate=pl.CostEstimate(
            flops=30 * work, bytes_accessed=10 * work, transcendentals=2 * work
        ),
    )(starts, *scalars, vir_row, acc, r_vector, r_previous, *held, *codes)


def next_kernel(acc_ref, rest_ref, r_ref, out_ref):
    for v in range(r_ref.shape[0] // O):
        rows = pl.ds(v * O, O)
        alpha = acc_ref[SUMS * v, 0:1, 0:1]
        scale = 1.0 / acc_ref[SUMS * v, 1:2, 0:1]
        value = rest_ref[rows, :] - alpha * r_ref[rows, :].astype(jnp.float32)
        out_ref[rows, :] = (value * scale).astype(out_ref.dtype)


def next_rows(acc, rest, r_vector, width):
    local_rows, row_width = r_vector.shape
    block = pl.BlockSpec((local_rows, width), lambda i: (0, i))
    return pl.pallas_call(
        next_kernel,
        grid=(row_width // width,),
        in_specs=[
            pl.BlockSpec(acc.shape, lambda i: (0, 0, 0)),
            block,
            block,
        ],
        out_specs=block,
        out_shape=jax.ShapeDtypeStruct((local_rows, row_width), jnp.bfloat16),
        compiler_params=pltpu.CompilerParams(vmem_limit_bytes=58 * 1024 * 1024),
        cost_estimate=pl.CostEstimate(
            flops=6 * local_rows * row_width,
            bytes_accessed=8 * local_rows * row_width,
            transcendentals=0,
        ),
    )(acc, rest, r_vector)


def streamed(
    r_vector, r_previous, cycle_block, ladder_block, occ_energy, vir_energy, beta_previous
):
    n_row = lax.axis_size("row")
    n_col = lax.axis_size("col")
    n_chip = n_col // CORES
    local_rows, row_width = r_vector.shape
    vectors = local_rows // O
    depth = row_width // n_row
    out_width = cycle_block.shape[1]
    j_part = ladder_block.shape[1]
    q_part = ladder_block.shape[3]
    row_at = lax.axis_index("row")
    col_at = lax.axis_index("col")
    chip_at = col_at // CORES
    core_at = col_at % CORES
    order = list(range(0, n_chip, 2)) + list(range(1, n_chip, 2))[::-1]
    place = [order.index(chip) for chip in range(n_chip)]
    paired = n_row & (n_row - 1) == 0

    def partner(row, m):
        return row ^ m if paired else (row + m) % n_row

    def back(row, m):
        return row ^ m if paired else (row + n_row - m) % n_row

    def send(value, rows=0, hops=0, swap=0, reverse=False, route=None, near=None):
        pairs = []
        for row in range(n_row):
            for chip in range(n_chip):
                for core in range(CORES):
                    to_row = back(row, rows) if reverse else partner(row, rows)
                    to_chip = route[chip] if route else order[(place[chip] + hops) % n_chip]
                    if near is not None and near != (abs(to_chip - chip) <= 1):
                        continue
                    to_core = (core + swap) % CORES
                    pairs.append(
                        (
                            row * n_col + chip * CORES + core,
                            to_row * n_col + to_chip * CORES + to_core,
                        )
                    )
        return lax.ppermute(value, AXES, pairs)

    other_block = send(cycle_block, swap=1)
    r_float = r_vector.astype(jnp.float32)
    rr_sum = jnp.sum(r_float.reshape(vectors, O * row_width) ** 2, axis=1)
    exponent = jnp.clip(jnp.floor(0.5 * jnp.log2(jnp.maximum(rr_sum, 1e-37))), -60.0, 60.0)
    shrink = jnp.repeat(power_of_two(-exponent), O)
    grow = power_of_two(exponent).astype(jnp.float32)

    def own_part(m):
        at = partner(row_at, m) * depth
        source = r_vector if m < 2 else after(r_vector, mine[0, 0])
        return lax.dynamic_slice_in_dim(source, at, depth, axis=1) * shrink[:, None]

    mine = {(0, 0): own_part(0)}
    for m in range(1, n_row):
        part = own_part(m)
        if m == n_row - 1 and m > 2:
            part = after(part, mine[0, 1], mine[0, 2])
        mine[0, m] = send(part, rows=m)
    ladder_rows = after(ladder_block, mine[0, 1]).transpose(1, 0, 3, 2).reshape(j_part * O, q_part * O)
    ladder_rows = jnp.concatenate([ladder_rows, send(ladder_rows, swap=1)], axis=0)
    turns = []
    for s in range(n_chip):
        if s < 2:
            turn = list(range(n_row))
        else:
            turn = list(range(1, n_row)) + [0]
        turns += [(s, m) for m in turn]
    owner_sends = []
    for chip in range(n_chip):
        before = order[(place[chip] + n_chip - 1) % n_chip]
        owner = order[(place[chip] + 1) % n_chip]
        owner_sends.append((owner, chip, True) if abs(owner - chip) < abs(before - chip) else (before, chip, False))
    nearest = n_chip > 2 and len({source for source, _, _ in owner_sends}) == n_chip
    route = {source: chip for source, chip, _ in owner_sends}
    as_owner = jnp.array(
        [own for source in range(n_chip) for at, _, own in owner_sends if at == source][:n_chip]
        if nearest
        else [False] * n_chip
    )[chip_at]
    def pass_on(g, *earlier):
        s, m = turns[g]
        part = mine[s - 1, m]
        if s == n_chip - 1 and nearest:
            part = jnp.where(as_owner, mine[0, m], part)
        lag = 2 if s == n_chip - 1 else 3
        if g - lag >= n_row:
            earlier += (mine[turns[g - lag]],)
        if earlier:
            part = after(part, *earlier)
        if s == n_chip - 1 and nearest:
            mine[s, m] = send(part, route=route)
        else:
            mine[s, m] = send(part, hops=1)

    order_table = jnp.array(order, dtype=jnp.int32)
    place_at = jnp.array(place, dtype=jnp.int32)[chip_at]
    starts = []
    for s in range(n_chip):
        for swap in range(CORES):
            chip = order_table[(place_at + s) % n_chip]
            starts.append((chip * CORES + (core_at + swap) % CORES) * out_width)
    starts = jnp.stack(starts)
    linear_index = row_at * n_col + col_at
    beta_here = lax.dynamic_slice_in_dim(beta_previous, linear_index * vectors, vectors)
    scalars = (occ_energy, grow, rr_sum, beta_here)

    groups = []
    for s in range(n_chip):
        turn = [(s, m) for m in list(range(1, n_row)) + [0]]
        if s < n_chip - 1:
            groups += [turn[k : k + 2] for k in range(0, n_row, 2)]
        else:
            groups += [turn[:2]] + [[at] for at in turn[2:]]
    last_of = {group[0][0]: g for g, group in enumerate(groups)}
    parts = {}
    arrived = {}
    codes = {}

    def summed(s):
        total = parts[s, 0]
        for k in range(1, n_row):
            total = total + decode(arrived[s, k], PART_GAIN)
        return encode(total, SUM_GAIN)

    sent = n_row
    while sent < min(2 * n_row, len(turns)):
        pass_on(sent, *([other_block] if sent == 2 * n_row - 1 else []))
        sent += 1
    acc = jnp.zeros((vectors * SUMS, 8, V), jnp.float32)
    vir_row = vir_energy[None, :]
    start_early, start_late = starts[: CORES * (n_chip - 1)], starts[CORES * (n_chip - 1) :]
    for g, group in enumerate(groups):
        s = group[0][0]
        earlier = []
        if g > 0:
            earlier.append(parts[groups[g - 1][0]])
        if g > 1:
            earlier += [arrived[at] for at in groups[g - 2] if at in arrived]
        for k in range(n_chip - 1):
            if last_of[k] + (2 if k < n_chip - 2 else 1) == g:
                code = summed(k)
                earlier.append(code)
                if k == 0:
                    codes[k] = code
                elif k < n_chip - 2:
                    codes[k] = send(code, hops=n_chip - k)
                else:
                    near_code = send(code, hops=n_chip - k, near=True)
                    far_code = code
        if n_row + g + 1 < sent and 0 < g <= n_row:
            earlier.append(mine[turns[n_row + g + 1]])
        if g == len(groups) - 2 and n_chip > 2:
            earlier.append(near_code)
        for k in range(1, n_chip - 1):
            if k in codes and k < n_chip - 2 and g == last_of[k] + 4:
                earlier.append(codes[k])
        while any(at not in mine for at in group):
            pass_on(sent)
            sent += 1
        pieces = [mine[at] for at in group]
        if g == 0:
            pieces[0], start_early, start_late, vir_row, acc, *scalars = lax.optimization_barrier(
                (pieces[0], start_early, start_late, vir_row, acc, *scalars)
            )
        if earlier:
            pieces[0] = after(pieces[0], *earlier)
        made = product(pieces, cycle_block, other_block, ladder_rows, [m != 0 for _, m in group])
        for at, part in zip(group, made):
            parts[at] = part
            if at[1] != 0:
                arrived[at] = send(part, rows=at[1], reverse=True)
        if sent < len(turns):
            pass_on(sent, made[0])
            sent += 1
        if sent < len(turns) and g >= len(groups) - n_row - 1:
            pass_on(sent)
            sent += 1
    s = n_chip - 1
    code = summed(s)
    if n_chip > 2:
        far_code = after(far_code, mine[turns[-2]])
        far_code = send(far_code, hops=2, near=False)
        code = after(code, far_code)
        codes[n_chip - 2] = near_code + far_code
    codes[s] = send(code, hops=n_chip - s)
    early = [codes[k] for k in range(n_chip - 1)]
    late = [codes[s]]
    early[0] = after(early[0], code)
    rest, acc = add_sums(
        early, start_early, False, scalars, vir_row, acc, None, r_vector, r_previous
    )
    rest, acc = add_sums(
        late, start_late, True, scalars, vir_row, acc, rest, r_vector, r_previous
    )
    next_vector = next_rows(acc, rest, r_vector, CORES * out_width)
    both = acc.reshape(vectors, SUMS, 8, V)[:, 0, :2, 0].T
    whole = lax.dynamic_update_slice(
        jnp.zeros((2, NVEC), jnp.float32), both, (0, linear_index * vectors)
    )
    whole = whole + send(whole, swap=1)
    for group in ([{"hops": h} for h in range(1, n_chip)], [{"rows": m} for m in range(1, n_row)]):
        whole = sum([send(whole, **kind) for kind in group], whole)
    return (next_vector, whole[0], whole[1])


def gathered(
    r_vector, r_previous, cycle_block, ladder_block, occ_energy, vir_energy, beta_previous
):
    n_row = lax.axis_size("row")
    n_col = lax.axis_size("col")
    local_rows = r_vector.shape[0]
    row_width = r_vector.shape[1]
    all_rows = NVEC * O
    j_part = ladder_block.shape[1]
    q_part = ladder_block.shape[3]
    column_part = lax.all_to_all(r_vector, "row", split_axis=1, concat_axis=0, tiled=True)
    shaped = column_part.reshape(n_row, 1, local_rows, column_part.shape[1])
    gathered = lax.all_gather(shaped, "col", axis=1, tiled=True)
    operand = gathered.reshape(all_rows, column_part.shape[1])
    cycle_part = jnp.dot(operand, cycle_block, preferred_element_type=jnp.float32)
    ladder_part = jnp.einsum(
        "ijpq,npqa->nija",
        ladder_block,
        operand.reshape(NVEC, O, q_part, V),
        preferred_element_type=jnp.float32,
    )
    out_width = j_part * V
    partial_value = cycle_part + ladder_part.reshape(all_rows, out_width)
    summed = lax.psum_scatter(
        partial_value.reshape(n_row, n_col, local_rows, out_width),
        "row",
        scatter_dimension=0,
        tiled=True,
    )
    sigma_rows = lax.all_to_all(summed, "col", split_axis=1, concat_axis=3, tiled=True)
    sigma_rows = sigma_rows.reshape(local_rows, row_width)
    linear_index = lax.axis_index("row") * n_col + lax.axis_index("col")
    row_ids = linear_index * local_rows + jnp.arange(local_rows, dtype=jnp.int32)
    occ_index = row_ids % O
    vec_of_row = row_ids // O
    occ_rows = jnp.sum(
        jnp.where(occ_index[:, None] == jnp.arange(O)[None, :], occ_energy[None, :], 0.0), axis=1
    )
    r_float = r_vector.astype(jnp.float32)
    prev_float = r_previous.astype(jnp.float32)
    diagonal = vir_energy[None, None, :] - occ_rows[:, None, None] - occ_energy[None, :, None]
    sigma_rows = sigma_rows + (diagonal * r_float.reshape(local_rows, O, V)).reshape(
        local_rows, row_width
    )
    member = (vec_of_row[:, None] == jnp.arange(NVEC)[None, :]).astype(jnp.float32)
    count_all = O * O * V

    def per_vector(row_sums):
        return jnp.sum(member * row_sums[:, None], axis=0)

    def per_row(coefs):
        return jnp.sum(member * coefs[None, :], axis=1)

    ss_sum, rs_sum, rr_sum, sp_sum, rp_sum, pp_sum = lax.psum(
        (
            per_vector(jnp.sum(sigma_rows * sigma_rows, axis=1)),
            per_vector(jnp.sum(r_float * sigma_rows, axis=1)),
            per_vector(jnp.sum(r_float * r_float, axis=1)),
            per_vector(jnp.sum(prev_float * sigma_rows, axis=1)),
            per_vector(jnp.sum(r_float * prev_float, axis=1)),
            per_vector(jnp.sum(prev_float * prev_float, axis=1)),
        ),
        AXES,
    )
    alpha_coef = rs_sum / count_all / (rr_sum / count_all + 1e-06)
    norm_sum = (
        ss_sum
        - 2.0 * alpha_coef * rs_sum
        - 2.0 * beta_previous * sp_sum
        + alpha_coef * alpha_coef * rr_sum
        + 2.0 * alpha_coef * beta_previous * rp_sum
        + beta_previous * beta_previous * pp_sum
    )
    residual_vec = (
        sigma_rows
        - per_row(alpha_coef)[:, None] * r_float
        - per_row(beta_previous)[:, None] * prev_float
    )
    beta_coef = jnp.sqrt(norm_sum / count_all + 1e-06)
    next_vector = (residual_vec / per_row(beta_coef)[:, None]).astype(jnp.bfloat16)
    return (next_vector, alpha_coef, beta_coef)


def on_device(r_vector, *others):
    whole_vectors = r_vector.shape[0] % O == 0 and lax.axis_size("col") % CORES == 0
    body = streamed if whole_vectors else gathered
    return body(r_vector, *others)


def solution(mesh):
    placed = (
        P(AXES, None),
        P(AXES, None),
        P("row", "col"),
        P(None, "col", None, "row"),
        P(),
        P(),
        P(),
    )
    return jax.shard_map(
        on_device,
        mesh=mesh,
        in_specs=placed,
        out_specs=(P(AXES, None), P(), P()),
        check_vma=False,
    )
```

```python
import functools

import jax
import jax.numpy as jnp
from jax import lax
from jax.experimental import pallas as pl
from jax.experimental.pallas import tpu as pltpu
from jax.sharding import PartitionSpec as P

O = 48
V = 384
NVEC = 64
CORES = 2
AXES = ("row", "col")
POWER = 16
FLOOR = 2.0**-7.75
PART_GAIN = 16.0
SUM_GAIN = 8.0


def encode(value, gain):
    size = jnp.abs(value) * gain + FLOOR
    size = size * size
    size = size * size
    size = size * size
    size = size * size
    return jnp.where(value < 0, -size, size).astype(jnp.bfloat16)


def decode(code, gain):
    wide = code.astype(jnp.float32)
    size = (jnp.exp2(jnp.log2(jnp.abs(wide)) * (1.0 / POWER)) - FLOOR) * (1.0 / gain)
    return jnp.where(wide < 0, -size, size)


def product_kernel(coded, *refs):
    count = len(coded)
    parts = refs[:count]
    own_ref, other_ref, ladder_ref = refs[count : count + 3]
    outs = refs[count + 3 : 2 * count + 3]
    rows_buf, cycle_buf, ladder_buf, sems, row_sems = refs[2 * count + 3 :]
    local_rows, depth = parts[0].shape
    slots, _, width = cycle_buf.shape
    blocks = own_ref.shape[1] // width
    q_part = depth // V
    j_part = ladder_ref.shape[0] // O

    def cycle_copy(half, b):
        at = pl.multiple_of(b * width, width)
        slot = lax.rem(half * blocks + b, slots)
        return pltpu.make_async_copy(
            (other_ref if half else own_ref).at[:, pl.ds(at, width)],
            cycle_buf.at[slot],
            sems.at[slot],
        )

    def start(b):
        @pl.when(b < blocks)
        def _():
            cycle_copy(0, b).start()

        @pl.when((b >= blocks) & (b < CORES * blocks))
        def _():
            cycle_copy(1, b - blocks).start()

    copies = [
        pltpu.make_async_copy(part, rows_buf.at[pl.ds(k * local_rows, local_rows)], row_sems.at[k])
        for k, part in enumerate(parts)
    ]
    for copy in copies:
        copy.start()
    for b in range(slots - 1):
        start(jnp.int32(b))
    for copy in copies:
        copy.wait()
    for n in range(count * local_rows // O):
        stacked = jnp.concatenate(
            [rows_buf[n * O : (n + 1) * O, q * V : (q + 1) * V] for q in range(q_part)], axis=0
        )
        term = jnp.dot(ladder_ref[...], stacked, preferred_element_type=jnp.float32)
        for j in range(j_part):
            ladder_buf[n * O : (n + 1) * O, j * V : (j + 1) * V] = term[j * O : (j + 1) * O]

    @pl.loop(0, CORES * blocks)
    def _(b):
        start(b + slots - 1)
        slot = lax.rem(b, slots)
        pltpu.make_async_copy(
            own_ref.at[:, pl.ds(0, width)], cycle_buf.at[slot], sems.at[slot]
        ).wait()
        columns = pl.ds(pl.multiple_of(b * width, width), width)
        value = jnp.dot(rows_buf[...], cycle_buf[slot], preferred_element_type=jnp.float32)
        value = value + ladder_buf[:, columns]
        for k in range(count):
            piece = value[k * local_rows : (k + 1) * local_rows]
            outs[k][:, columns] = encode(piece, PART_GAIN) if coded[k] else piece


def product(parts, cycle_block, other_block, ladder_rows, coded):
    local_rows, depth = parts[0].shape
    out_width = CORES * cycle_block.shape[1]
    width = 2 * V if cycle_block.shape[1] % (2 * V) == 0 else V
    count = len(parts)
    rows = count * local_rows
    slots = 3
    hbm = pl.BlockSpec(memory_space=pl.ANY)
    vmem = pl.BlockSpec(memory_space=pltpu.VMEM)
    return pl.pallas_call(
        functools.partial(product_kernel, coded),
        in_specs=[hbm] * (count + 2) + [vmem],
        out_specs=[vmem] * count,
        out_shape=[
            jax.ShapeDtypeStruct((local_rows, out_width), jnp.bfloat16 if c else jnp.float32)
            for c in coded
        ],
        scratch_shapes=[
            pltpu.VMEM((rows, depth), jnp.bfloat16),
            pltpu.VMEM((slots, depth, width), jnp.bfloat16),
            pltpu.VMEM((rows, out_width), jnp.float32),
            pltpu.SemaphoreType.DMA((slots,)),
            pltpu.SemaphoreType.DMA((count,)),
        ],
        compiler_params=pltpu.CompilerParams(vmem_limit_bytes=48 * 1024 * 1024),
        cost_estimate=pl.CostEstimate(
            flops=2 * rows * out_width, bytes_accessed=2 * rows * out_width, transcendentals=0
        ),
    )(*parts, cycle_block, other_block, ladder_rows)


def power_of_two(exponent):
    return jnp.exp2(exponent).astype(jnp.bfloat16)


def after(value, *earlier):
    return lax.optimization_barrier((value,) + earlier)[0]


SUMS = 3


def sums_kernel(blocks, last, starts, occ, grow, rr, beta_prev, vir_ref, acc_in, r_ref, prev_ref, *refs):
    refs = refs[1:] if last else refs
    codes = refs[: blocks // CORES]
    rest_ref, acc_ref, code_buf, r_buf, prev_buf, rest_buf, sems = refs[blocks // CORES :]
    local_rows, row_width = r_ref.shape
    out_width = codes[0].shape[1] // CORES
    vectors = local_rows // O
    count_all = float(O * O * V)
    copies = []
    outward = []
    for b in range(blocks):
        columns = pl.ds(pl.multiple_of(starts[b], out_width), out_width)
        copies.append(
            [
                pltpu.make_async_copy(
                    codes[b // CORES].at[:, pl.ds(b % CORES * out_width, out_width)],
                    code_buf.at[b],
                    sems.at[0, b],
                ),
                pltpu.make_async_copy(r_ref.at[:, columns], r_buf.at[b], sems.at[1, b]),
                pltpu.make_async_copy(prev_ref.at[:, columns], prev_buf.at[b], sems.at[2, b]),
            ]
        )
        outward.append(
            pltpu.make_async_copy(rest_buf.at[b], rest_ref.at[:, columns], sems.at[3, b])
        )
    for group in copies:
        for copy in group:
            copy.start()
    occ_column = lax.broadcasted_iota(jnp.int32, (O, 1), 0)
    occ_rows = jnp.zeros((O, 1), jnp.float32)
    for i in range(O):
        occ_rows = jnp.where(occ_column == i, occ[i], occ_rows)
    base = vir_ref[...] - occ_rows
    acc_ref[...] = acc_in[...]

    def folded(value):
        return jnp.sum(value.reshape(O // 8, 8, V), axis=0)

    for b in range(blocks):
        for copy in copies[b]:
            copy.wait()

        @pl.loop(0, out_width // V)
        def _(j):
            columns = pl.ds(pl.multiple_of(j * V, V), V)
            level = base - occ[starts[b] // V + j]
            for v in range(vectors):
                rows = pl.ds(v * O, O)
                r = r_buf[b, rows, columns].astype(jnp.float32)
                p = prev_buf[b, rows, columns].astype(jnp.float32)
                value = decode(code_buf[b, rows, columns], SUM_GAIN) * grow[v] + level * r
                rest = value - beta_prev[v] * p
                rest_buf[b, rows, columns] = rest
                for k, term in enumerate((rest * rest, value * r, rest * r)):
                    acc_ref[SUMS * v + k] += folded(term)

        outward[b].start()
    if last:
        for v in range(vectors):
            tt, rs, tr = [
                jnp.full((1, 128), jnp.sum(acc_ref[SUMS * v + k])) for k in range(SUMS)
            ]
            alpha = rs / count_all / (rr[v] / count_all + 1e-06)
            norm = tt - 2.0 * alpha * tr + alpha * alpha * rr[v]
            acc_ref[SUMS * v, 0:1, 0:128] = alpha
            acc_ref[SUMS * v, 1:2, 0:128] = jnp.sqrt(norm / count_all + 1e-06)
    for copy in outward:
        copy.wait()


def add_sums(codes, starts, last, scalars, vir_row, acc, rest, r_vector, r_previous):
    local_rows, row_width = r_vector.shape
    blocks = CORES * len(codes)
    out_width = codes[0].shape[1] // CORES
    smem = pl.BlockSpec(memory_space=pltpu.SMEM)
    hbm = pl.BlockSpec(memory_space=pl.ANY)
    vmem = pl.BlockSpec(memory_space=pltpu.VMEM)
    work = blocks * local_rows * out_width
    held = [rest] if last else []
    return pl.pallas_call(
        functools.partial(sums_kernel, blocks, last),
        in_specs=[smem] * 5 + [vmem] * 2 + [hbm] * (2 + len(held) + len(codes)),
        out_specs=(hbm, vmem),
        out_shape=(
            jax.ShapeDtypeStruct((local_rows, row_width), jnp.float32),
            jax.ShapeDtypeStruct(acc.shape, jnp.float32),
        ),
        scratch_shapes=[
            pltpu.VMEM((blocks, local_rows, out_width), jnp.bfloat16),
            pltpu.VMEM((blocks, local_rows, out_width), jnp.bfloat16),
            pltpu.VMEM((blocks, local_rows, out_width), jnp.bfloat16),
            pltpu.VMEM((blocks, local_rows, out_width), jnp.float32),
            pltpu.SemaphoreType.DMA((4, blocks)),
        ],
        input_output_aliases={9: 0} if last else {},
        compiler_params=pltpu.CompilerParams(vmem_limit_bytes=58 * 1024 * 1024),
        cost_estimate=pl.CostEstimate(
            flops=30 * work, bytes_accessed=10 * work, transcendentals=2 * work
        ),
    )(starts, *scalars, vir_row, acc, r_vector, r_previous, *held, *codes)


def next_kernel(acc_ref, rest_ref, r_ref, out_ref):
    for v in range(r_ref.shape[0] // O):
        rows = pl.ds(v * O, O)
        alpha = acc_ref[SUMS * v, 0:1, 0:1]
        scale = 1.0 / acc_ref[SUMS * v, 1:2, 0:1]
        value = rest_ref[rows, :] - alpha * r_ref[rows, :].astype(jnp.float32)
        out_ref[rows, :] = (value * scale).astype(out_ref.dtype)


def next_rows(acc, rest, r_vector, width):
    local_rows, row_width = r_vector.shape
    block = pl.BlockSpec((local_rows, width), lambda i: (0, i))
    return pl.pallas_call(
        next_kernel,
        grid=(row_width // width,),
        in_specs=[
            pl.BlockSpec(acc.shape, lambda i: (0, 0, 0)),
            block,
            block,
        ],
        out_specs=block,
        out_shape=jax.ShapeDtypeStruct((local_rows, row_width), jnp.bfloat16),
        compiler_params=pltpu.CompilerParams(vmem_limit_bytes=58 * 1024 * 1024),
        cost_estimate=pl.CostEstimate(
            flops=6 * local_rows * row_width,
            bytes_accessed=8 * local_rows * row_width,
            transcendentals=0,
        ),
    )(acc, rest, r_vector)


def streamed(
    r_vector, r_previous, cycle_block, ladder_block, occ_energy, vir_energy, beta_previous
):
    n_row = lax.axis_size("row")
    n_col = lax.axis_size("col")
    n_chip = n_col // CORES
    local_rows, row_width = r_vector.shape
    vectors = local_rows // O
    depth = row_width // n_row
    out_width = cycle_block.shape[1]
    j_part = ladder_block.shape[1]
    q_part = ladder_block.shape[3]
    row_at = lax.axis_index("row")
    col_at = lax.axis_index("col")
    chip_at = col_at // CORES
    core_at = col_at % CORES
    order = list(range(0, n_chip, 2)) + list(range(1, n_chip, 2))[::-1]
    place = [order.index(chip) for chip in range(n_chip)]
    paired = n_row & (n_row - 1) == 0

    def partner(row, m):
        return row ^ m if paired else (row + m) % n_row

    def back(row, m):
        return row ^ m if paired else (row + n_row - m) % n_row

    def send(value, rows=0, hops=0, swap=0, reverse=False, route=None, near=None):
        pairs = []
        for row in range(n_row):
            for chip in range(n_chip):
                for core in range(CORES):
                    to_row = back(row, rows) if reverse else partner(row, rows)
                    to_chip = route[chip] if route else order[(place[chip] + hops) % n_chip]
                    if near is not None and near != (abs(to_chip - chip) <= 1):
                        continue
                    to_core = (core + swap) % CORES
                    pairs.append(
                        (
                            row * n_col + chip * CORES + core,
                            to_row * n_col + to_chip * CORES + to_core,
                        )
                    )
        return lax.ppermute(value, AXES, pairs)

    other_block = send(cycle_block, swap=1)
    r_float = r_vector.astype(jnp.float32)
    rr_sum = jnp.sum(r_float.reshape(vectors, O * row_width) ** 2, axis=1)
    exponent = jnp.clip(jnp.floor(0.5 * jnp.log2(jnp.maximum(rr_sum, 1e-37))), -60.0, 60.0)
    shrink = jnp.repeat(power_of_two(-exponent), O)
    grow = power_of_two(exponent).astype(jnp.float32)

    def own_part(m):
        at = partner(row_at, m) * depth
        source = r_vector if m < 2 else after(r_vector, mine[0, 0])
        return lax.dynamic_slice_in_dim(source, at, depth, axis=1) * shrink[:, None]

    mine = {(0, 0): own_part(0)}
    for m in range(1, n_row):
        part = own_part(m)
        if m == n_row - 1 and m > 2:
            part = after(part, mine[0, 1], mine[0, 2])
        mine[0, m] = send(part, rows=m)
    ladder_rows = after(ladder_block, mine[0, 1]).transpose(1, 0, 3, 2).reshape(j_part * O, q_part * O)
    ladder_rows = jnp.concatenate([ladder_rows, send(ladder_rows, swap=1)], axis=0)
    turns = []
    for s in range(n_chip):
        if s < 2:
            turn = list(range(n_row))
        else:
            turn = list(range(1, n_row)) + [0]
        turns += [(s, m) for m in turn]
    owner_sends = []
    for chip in range(n_chip):
        before = order[(place[chip] + n_chip - 1) % n_chip]
        owner = order[(place[chip] + 1) % n_chip]
        owner_sends.append((owner, chip, True) if abs(owner - chip) < abs(before - chip) else (before, chip, False))
    nearest = n_chip > 2 and len({source for source, _, _ in owner_sends}) == n_chip
    route = {source: chip for source, chip, _ in owner_sends}
    as_owner = jnp.array(
        [own for source in range(n_chip) for at, _, own in owner_sends if at == source][:n_chip]
        if nearest
        else [False] * n_chip
    )[chip_at]
    def pass_on(g, *earlier):
        s, m = turns[g]
        part = mine[s - 1, m]
        if s == n_chip - 1 and nearest:
            part = jnp.where(as_owner, mine[0, m], part)
        lag = 2 if s == n_chip - 1 else 3
        if g - lag >= n_row:
            earlier += (mine[turns[g - lag]],)
        if earlier:
            part = after(part, *earlier)
        if s == n_chip - 1 and nearest:
            mine[s, m] = send(part, route=route)
        else:
            mine[s, m] = send(part, hops=1)

    order_table = jnp.array(order, dtype=jnp.int32)
    place_at = jnp.array(place, dtype=jnp.int32)[chip_at]
    starts = []
    for s in range(n_chip):
        for swap in range(CORES):
            chip = order_table[(place_at + s) % n_chip]
            starts.append((chip * CORES + (core_at + swap) % CORES) * out_width)
    starts = jnp.stack(starts)
    linear_index = row_at * n_col + col_at
    beta_here = lax.dynamic_slice_in_dim(beta_previous, linear_index * vectors, vectors)
    scalars = (occ_energy, grow, rr_sum, beta_here)

    groups = []
    for s in range(n_chip):
        turn = [(s, m) for m in list(range(1, n_row)) + [0]]
        if s < n_chip - 1:
            groups += [turn[k : k + 2] for k in range(0, n_row, 2)]
        else:
            groups += [turn[:2]] + [[at] for at in turn[2:]]
    last_of = {group[0][0]: g for g, group in enumerate(groups)}
    parts = {}
    arrived = {}
    codes = {}

    def summed(s):
        total = parts[s, 0]
        for k in range(1, n_row):
            total = total + decode(arrived[s, k], PART_GAIN)
        return encode(total, SUM_GAIN)

    sent = n_row
    while sent < min(2 * n_row, len(turns)):
        pass_on(sent, *([other_block] if sent == 2 * n_row - 1 else []))
        sent += 1
    acc = jnp.zeros((vectors * SUMS, 8, V), jnp.float32)
    vir_row = vir_energy[None, :]
    start_early, start_late = starts[: CORES * (n_chip - 1)], starts[CORES * (n_chip - 1) :]
    for g, group in enumerate(groups):
        s = group[0][0]
        earlier = []
        if g > 0:
            earlier.append(parts[groups[g - 1][0]])
        if g > 1:
            earlier += [arrived[at] for at in groups[g - 2] if at in arrived]
        for k in range(n_chip - 1):
            if last_of[k] + (2 if k < n_chip - 2 else 1) == g:
                code = summed(k)
                earlier.append(code)
                if k == 0:
                    codes[k] = code
                elif k < n_chip - 2:
                    codes[k] = send(code, hops=n_chip - k)
                else:
                    near_code = send(code, hops=n_chip - k, near=True)
                    far_code = code
        if n_row + g + 1 < sent and 0 < g <= n_row:
            earlier.append(mine[turns[n_row + g + 1]])
        if g == len(groups) - 2 and n_chip > 2:
            earlier.append(near_code)
        for k in range(1, n_chip - 1):
            if k in codes and k < n_chip - 2 and g == last_of[k] + 4:
                earlier.append(codes[k])
        while any(at not in mine for at in group):
            pass_on(sent)
            sent += 1
        pieces = [mine[at] for at in group]
        if g == 0:
            pieces[0], start_early, start_late, vir_row, acc, *scalars = lax.optimization_barrier(
                (pieces[0], start_early, start_late, vir_row, acc, *scalars)
            )
        if earlier:
            pieces[0] = after(pieces[0], *earlier)
        made = product(pieces, cycle_block, other_block, ladder_rows, [m != 0 for _, m in group])
        for at, part in zip(group, made):
            parts[at] = part
            if at[1] != 0:
                arrived[at] = send(part, rows=at[1], reverse=True)
        if sent < len(turns):
            pass_on(sent, made[0])
            sent += 1
        if sent < len(turns) and g >= len(groups) - n_row - 1:
            pass_on(sent)
            sent += 1
    s = n_chip - 1
    code = summed(s)
    if n_chip > 2:
        far_code = after(far_code, mine[turns[-2]])
        far_code = send(far_code, hops=2, near=False)
        code = after(code, far_code)
        codes[n_chip - 2] = near_code + far_code
    codes[s] = send(code, hops=n_chip - s)
    early = [codes[k] for k in range(n_chip - 1)]
    late = [codes[s]]
    early[0] = after(early[0], code)
    rest, acc = add_sums(
        early, start_early, False, scalars, vir_row, acc, None, r_vector, r_previous
    )
    rest, acc = add_sums(
        late, start_late, True, scalars, vir_row, acc, rest, r_vector, r_previous
    )
    next_vector = next_rows(acc, rest, r_vector, CORES * out_width)
    both = acc.reshape(vectors, SUMS, 8, V)[:, 0, :2, 0].T
    whole = lax.dynamic_update_slice(
        jnp.zeros((2, NVEC), jnp.float32), both, (0, linear_index * vectors)
    )
    whole = whole + send(whole, swap=1)
    for group in ([{"hops": h} for h in range(1, n_chip)], [{"rows": m} for m in range(1, n_row)]):
        whole = sum([send(whole, **kind) for kind in group], whole)
    return (next_vector, whole[0], whole[1])


def gathered(
    r_vector, r_previous, cycle_block, ladder_block, occ_energy, vir_energy, beta_previous
):
    n_row = lax.axis_size("row")
    n_col = lax.axis_size("col")
    local_rows = r_vector.shape[0]
    row_width = r_vector.shape[1]
    all_rows = NVEC * O
    j_part = ladder_block.shape[1]
    q_part = ladder_block.shape[3]
    column_part = lax.all_to_all(r_vector, "row", split_axis=1, concat_axis=0, tiled=True)
    shaped = column_part.reshape(n_row, 1, local_rows, column_part.shape[1])
    gathered = lax.all_gather(shaped, "col", axis=1, tiled=True)
    operand = gathered.reshape(all_rows, column_part.shape[1])
    cycle_part = jnp.dot(operand, cycle_block, preferred_element_type=jnp.float32)
    ladder_part = jnp.einsum(
        "ijpq,npqa->nija",
        ladder_block,
        operand.reshape(NVEC, O, q_part, V),
        preferred_element_type=jnp.float32,
    )
    out_width = j_part * V
    partial_value = cycle_part + ladder_part.reshape(all_rows, out_width)
    summed = lax.psum_scatter(
        partial_value.reshape(n_row, n_col, local_rows, out_width),
        "row",
        scatter_dimension=0,
        tiled=True,
    )
    sigma_rows = lax.all_to_all(summed, "col", split_axis=1, concat_axis=3, tiled=True)
    sigma_rows = sigma_rows.reshape(local_rows, row_width)
    linear_index = lax.axis_index("row") * n_col + lax.axis_index("col")
    row_ids = linear_index * local_rows + jnp.arange(local_rows, dtype=jnp.int32)
    occ_index = row_ids % O
    vec_of_row = row_ids // O
    occ_rows = jnp.sum(
        jnp.where(occ_index[:, None] == jnp.arange(O)[None, :], occ_energy[None, :], 0.0), axis=1
    )
    r_float = r_vector.astype(jnp.float32)
    prev_float = r_previous.astype(jnp.float32)
    diagonal = vir_energy[None, None, :] - occ_rows[:, None, None] - occ_energy[None, :, None]
    sigma_rows = sigma_rows + (diagonal * r_float.reshape(local_rows, O, V)).reshape(
        local_rows, row_width
    )
    member = (vec_of_row[:, None] == jnp.arange(NVEC)[None, :]).astype(jnp.float32)
    count_all = O * O * V

    def per_vector(row_sums):
        return jnp.sum(member * row_sums[:, None], axis=0)

    def per_row(coefs):
        return jnp.sum(member * coefs[None, :], axis=1)

    ss_sum, rs_sum, rr_sum, sp_sum, rp_sum, pp_sum = lax.psum(
        (
            per_vector(jnp.sum(sigma_rows * sigma_rows, axis=1)),
            per_vector(jnp.sum(r_float * sigma_rows, axis=1)),
            per_vector(jnp.sum(r_float * r_float, axis=1)),
            per_vector(jnp.sum(prev_float * sigma_rows, axis=1)),
            per_vector(jnp.sum(r_float * prev_float, axis=1)),
            per_vector(jnp.sum(prev_float * prev_float, axis=1)),
        ),
        AXES,
    )
    alpha_coef = rs_sum / count_all / (rr_sum / count_all + 1e-06)
    norm_sum = (
        ss_sum
        - 2.0 * alpha_coef * rs_sum
        - 2.0 * beta_previous * sp_sum
        + alpha_coef * alpha_coef * rr_sum
        + 2.0 * alpha_coef * beta_previous * rp_sum
        + beta_previous * beta_previous * pp_sum
    )
    residual_vec = (
        sigma_rows
        - per_row(alpha_coef)[:, None] * r_float
        - per_row(beta_previous)[:, None] * prev_float
    )
    beta_coef = jnp.sqrt(norm_sum / count_all + 1e-06)
    next_vector = (residual_vec / per_row(beta_coef)[:, None]).astype(jnp.bfloat16)
    return (next_vector, alpha_coef, beta_coef)


def on_device(r_vector, *others):
    whole_vectors = r_vector.shape[0] % O == 0 and lax.axis_size("col") % CORES == 0
    body = streamed if whole_vectors else gathered
    return body(r_vector, *others)


def solution(mesh):
    placed = (
        P(AXES, None),
        P(AXES, None),
        P("row", "col"),
        P(None, "col", None, "row"),
        P(),
        P(),
        P(),
    )
    return jax.shard_map(
        on_device,
        mesh=mesh,
        in_specs=placed,
        out_specs=(P(AXES, None), P(), P()),
        check_vma=False,
    )
```
